32 devices in a mesh: groups: 2 (over x), rows: 16 (over z, y, core).
Axes of the slice: x: 2, y: 2, z: 4, core: 2. Of those that a mesh axis runs over, the one named last changes fastest.
Arguments:
- embeddings: bfloat16 [65536, 768], P(('groups', 'rows')), parts along dimension 0, may hold values from -6 to 6
- cluster_id: int32 [65536, 1], P(('groups', 'rows')), parts along dimension 0, may hold values from 0 to 511; in each aligned block of 2048 rows (0 to 2047, 2048 to 4095, ...) at most 16 rows name the same one
Outputs:
- nearest: float32 [65536], P(('groups', 'rows')), parts along dimension 0
The draws below stay inside these ranges and needn't reach their ends.
There are 2 independent parts, one for each index of `groups`. The reference program is written for one: setup_inputs(seed, part) draws one part's arguments, and reference() takes and returns one part's arrays. A program takes and returns all parts, laid end to end along the dimension named above; each array names one. Nothing has to cross between parts.
Inputs may be any that keep to these rules, and one draw needn't show every extreme that they name: `cluster_id`: in each aligned block of 2048 rows (the rows of one device) no cluster is named by more than 16 rows, a bound that some block reaches; every cluster is named somewhere.
All inputs are finite; a program needn't handle non-finite values.
Results may differ from the reference program's by a relative error of at most 0.0018.
Values may be sent and summed in bfloat16 or wider, within the bound.
No kernel may reach another device: no remote copies, remote signals or barrier semaphores. Data moves between devices by JAX's collectives and lax.ppermute only.
A program may use at most 128 MiB of HBM per device.

```python
import math
import jax
import jax.numpy as jnp
import numpy as np
from jax import lax

E = 768
CLUSTERS = 512
MOST = 16
ROWS_DEV = 2048
ROWS = 32768
N_ROWS = 16


def levels(key, extent, cuts, smallest, largest):
    loudness, own = 1.0, jax.random.fold_in(key, 6)
    for axis_at, shards_of in cuts:
        heights = jnp.exp(jax.random.uniform(jax.random.fold_in(own, axis_at), (shards_of,), jnp.float32, smallest / len(cuts), largest / len(cuts)))
        loudness = loudness * jnp.repeat(heights, extent[axis_at] // shards_of).reshape([-1 if axis == axis_at else 1 for axis in range(len(extent))])
    return loudness


def shared_out(own_key, own, number, rows, count, top, most, lean):
    order = jax.random.permutation(own_key, count)
    heavy_load, usual = portions_of(count, rows * top, most, lean, True), portions_of(count, rows * top, most, lean, False)
    places = jnp.arange(count)

    def named(tallies, offset_by):
        used = int((tallies > 0).sum())
        fixed = max(1, used // 4)
        passed = fixed + (places - fixed + offset_by * (used - fixed)) % max(1, count - fixed)
        return jnp.zeros((count,), jnp.int32).at[order[jnp.where(places < fixed, places, passed)]].set(jnp.asarray(tallies, jnp.int32))

    tallies = jnp.where(number % 4 == 0, named(heavy_load, number // 4), named(usual, number - number // 4 - 1))
    mixed = jax.random.permutation(jax.random.fold_in(own, 3), count)
    giver, receiver = mixed[0:count // 2 * 2:2], mixed[1:count // 2 * 2:2]
    room = jnp.minimum(tallies[giver] - 1, most - tallies[receiver]) // 2
    room = jnp.where((giver == order[0]) | (receiver == order[0]) | (tallies[receiver] == 0), 0, jnp.maximum(room, 0))
    passed = jax.random.randint(jax.random.fold_in(own, 4), (count // 2,), 0, 1 << 20) % (room + 1)
    tallies = tallies.at[giver].add(-passed).at[receiver].add(passed)
    items = jnp.searchsorted(jnp.cumsum(tallies), jnp.arange(rows * top), side="right").astype(jnp.int32)
    grid = items.reshape(top, rows).T
    grid = grid[jax.random.permutation(jax.random.fold_in(own, 1), rows)]
    offset_by = jax.random.randint(jax.random.fold_in(own, 2), (rows, 1), 0, top)
    return jnp.take_along_axis(grid, (jnp.arange(top)[None, :] + offset_by) % top, axis=1)


def portions_of(count, total, limit, slope, full):
    loads = [(1 << 20) // math.isqrt(rank ** slope) + 1 for rank in range(1, count + 1)]
    largest = limit if full else min(limit, max(-(-total // count), total * loads[0] // sum(loads)))
    least = 1 if total - largest >= count - 1 else 0
    holding, rest = [largest] + [least] * (count - 1), total - largest - least * (count - 1)
    while rest > 0:
        free = [i for i in range(1, count) if holding[i] < largest] or [i for i in range(1, count) if holding[i] < limit]
        mass, left = sum([loads[i] for i in free]), rest
        for i in free:
            addition = min(limit - holding[i], max(1, left * loads[i] // mass), rest)
            holding[i] = holding[i] + addition
            rest = rest - addition
    return np.array(holding)


def bell_draw(own_key, shape, deviation, bound, pieces=(), kind=jnp.bfloat16):
    result = deviation * jax.random.normal(own_key, shape, jnp.float32)
    if pieces:
        result = result * levels(own_key, shape, pieces, -0.22, 0.18)
    return jnp.clip(result, -bound, bound).astype(kind)


def setup_inputs(seed: int = 0, part: int = 0) -> dict:
    seeds = jax.random.split(jax.random.key(seed), 3)
    part_splits = jax.random.split(jax.random.fold_in(seeds[2], part), 3)
    embeddings = bell_draw(part_splits[0], (ROWS, E), 1.0, 6.0, ((0, 16),))
    cluster_id_keys = jax.random.split(jax.random.fold_in(part_splits[1], 1), ROWS // ROWS_DEV)
    cluster_id_turns = jax.random.permutation(jax.random.fold_in(part_splits[1], 3), ROWS // ROWS_DEV)
    cluster_id = jax.vmap(lambda own, number: shared_out(jax.random.fold_in(part_splits[1], 2), own, number, ROWS_DEV, CLUSTERS, 1, MOST, 2))(cluster_id_keys, cluster_id_turns).reshape((ROWS, 1))
    return {"embeddings": embeddings, "cluster_id": cluster_id}


def reference(embeddings, cluster_id):
    labels = cluster_id[:, 0].astype(jnp.int32)
    count = labels.shape[0]
    capacity = N_ROWS * MOST
    values = embeddings.astype(jnp.float32)
    unit = (values * lax.rsqrt(lax.optimization_barrier(jnp.sum(values * values, axis=1, keepdims=True)) + 1e-06)).astype(jnp.bfloat16)
    order = jnp.argsort(labels, stable=True).astype(jnp.int32)
    sorted_labels = labels[order]
    first = jnp.searchsorted(sorted_labels, sorted_labels, side='left').astype(jnp.int32)
    ranks = jnp.zeros((count,), jnp.int32).at[order].set(jnp.arange(count, dtype=jnp.int32) - first)
    slot = labels * capacity + ranks
    members = jnp.full((CLUSTERS * capacity,), count, jnp.int32).at[slot].set(jnp.arange(count, dtype=jnp.int32))
    padded = jnp.concatenate([unit, jnp.zeros((1, unit.shape[1]), jnp.bfloat16)], axis=0)
    width = min(8, CLUSTERS)
    groups_of = members.reshape(CLUSTERS // width, width, capacity)
    diagonal = jnp.eye(capacity, dtype=bool)

    def per_block(index_block):
        block_rows = padded[index_block].astype(jnp.float32)
        gram = jnp.einsum('cie,cje->cij', block_rows, block_rows)
        valid = index_block < count
        keep = valid[:, None, :] & jnp.logical_not(diagonal)[None, :, :]
        return lax.optimization_barrier(jnp.max(jnp.where(keep, gram, jnp.float32(-1.0)), axis=2))
    best = lax.map(per_block, groups_of).reshape(CLUSTERS * capacity)
    return best[slot]
```

```python
import functools

import jax
import jax.numpy as jnp
from jax import lax
from jax.experimental import pallas as pl
from jax.experimental.pallas import tpu as pltpu
from jax.sharding import PartitionSpec as P

CLUSTERS = 512
MOST = 16
LANES = 128
SLACK = 32
EXACT = lax.Precision.HIGHEST
BF16, F32, I32 = jnp.bfloat16, jnp.float32, jnp.int32
VMEM_LIMIT = 48 * 1024 * 1024
NT = (((1,), (1,)), ((), ()))


def iota(shape, dim):
    return lax.broadcasted_iota(I32, shape, dim)


def one_hot(mask):
    return jnp.where(mask, jnp.float32(1), jnp.float32(0)).astype(BF16)


def whole(count):
    return [pl.BlockSpec(memory_space=pltpu.VMEM)] * count


def rank_kernel(label_ref, rank_ref, count_ref):
    step = 256
    tri = one_hot((iota((step, step + LANES), 0) < iota((step, step + LANES), 1)) | (iota((step, step + LANES), 1) >= step))
    ones = jnp.ones((count_ref.shape[0], step), BF16)
    running = jnp.zeros((CLUSTERS, LANES), F32)
    counts = jnp.zeros(count_ref.shape, F32)
    for at in range(0, label_ref.shape[1], step):
        hot = label_ref[:, at : at + step] == iota((CLUSTERS, step), 0)
        hot_bf = one_hot(hot)
        before = jnp.dot(hot_bf, tri, preferred_element_type=F32)
        here = before[:, :step] + jnp.concatenate([running] * (step // LANES), axis=1)
        rank_ref[:, at : at + step] = jnp.sum(jnp.where(hot, here, 0.0), axis=0, keepdims=True).astype(I32)
        running = running + before[:, step:]
        counts = counts + lax.dot_general(ones, hot_bf, NT, preferred_element_type=F32)
    count_ref[...] = counts


def ranks_and_counts(labels, peers):
    return pl.pallas_call(
        rank_kernel,
        out_shape=(
            jax.ShapeDtypeStruct(labels.shape, I32),
            jax.ShapeDtypeStruct((peers, CLUSTERS), F32),
        ),
        in_specs=whole(1),
        out_specs=tuple(whole(2)),
        name="ranks",
    )(labels)


def unit_kernel(rows_ref, unit_ref):
    values = rows_ref[...].astype(F32)
    total = jnp.sum(values * values, axis=1, keepdims=True)
    unit_ref[...] = (values * lax.rsqrt(total + 1e-06)).astype(BF16)


def unit_rows(embeddings):
    count, width = embeddings.shape
    step = min(512, count)
    spec = pl.BlockSpec((step, width), lambda i: (i, 0))
    return pl.pallas_call(
        unit_kernel,
        out_shape=jax.ShapeDtypeStruct((count, width), BF16),
        grid=(count // step,),
        in_specs=[spec],
        out_specs=spec,
        cost_estimate=pl.CostEstimate(flops=4 * count * width, bytes_accessed=4 * count * width, transcendentals=count),
        name="unit",
    )(embeddings)


def place_kernel(cap, me_ref, count_ref, label_ref, rank_ref, dest_ref, ends_ref, ends_t_ref, most_ref):
    me = me_ref[0]
    counts = count_ref[...]
    peers = counts.shape[0]
    square = (CLUSTERS, CLUSTERS)
    total = jnp.sum(counts, axis=0, keepdims=True)
    total_col = jnp.transpose(jnp.broadcast_to(total, (LANES, CLUSTERS)))[:, :1]
    first, second = iota(square, 0), iota(square, 1)
    ahead = (total_col > total) | ((total_col == total) & (first < second))
    ahead = jnp.where(ahead, jnp.float32(1), jnp.float32(0))
    turn = jnp.sum(ahead, axis=0, keepdims=True).astype(I32)
    turn_col = (CLUSTERS - 1) - jnp.sum(ahead, axis=1, keepdims=True).astype(I32)

    def owner_of(place):
        lap = place // peers
        spot = place - lap * peers
        return jnp.where(lap % 2 == 0, spot, peers - 1 - spot), lap

    owner, lap = owner_of(turn)
    owner_col, lap_col = owner_of(turn_col)
    earlier = one_hot((owner_col == owner) & (lap_col < lap))
    offset = jnp.dot(counts.astype(BF16), earlier, preferred_element_type=F32)
    ends = offset + counts
    most_ref[...] = jnp.broadcast_to(jnp.max(ends, axis=(0, 1), keepdims=True), most_ref.shape)

    mine = jnp.sum(jnp.where(iota(counts.shape, 0) == me, offset, 0.0), axis=0, keepdims=True).astype(I32)
    upper = mine // MOST
    table = jnp.concatenate([owner, upper, mine - upper * MOST] + [jnp.zeros_like(owner)] * 5, axis=0)
    table = table.astype(F32).astype(BF16)
    step = 512
    for at in range(0, label_ref.shape[1], step):
        hot = one_hot(label_ref[:, at : at + step] == iota((CLUSTERS, step), 0))
        found = jnp.dot(table, hot, preferred_element_type=F32).astype(I32)
        spot = found[1:2] * MOST + found[2:3] + rank_ref[:, at : at + step]
        dest_ref[:, at : at + step] = jnp.where(spot < cap, found[0:1] * cap + spot, -1)

    chosen = jnp.where((owner == me) & (lap == iota((LANES, CLUSTERS), 0)), jnp.float32(1), jnp.float32(0))
    never = jnp.float32(1 << 20)
    owned = CLUSTERS // peers
    own = lax.dot_general(ends, chosen, NT, precision=EXACT, preferred_element_type=F32)
    ends_ref[...] = jnp.where(iota(own.shape, 1) < owned, own, never)
    own_t = lax.dot_general(chosen, ends, NT, precision=EXACT, preferred_element_type=F32)
    ends_t_ref[...] = jnp.where(iota(own_t.shape, 0) < owned, own_t, never)


def places(me, counts, labels, ranks, cap):
    peers = counts.shape[0]
    return pl.pallas_call(
        functools.partial(place_kernel, cap),
        out_shape=(
            jax.ShapeDtypeStruct(labels.shape, I32),
            jax.ShapeDtypeStruct((peers, LANES), F32),
            jax.ShapeDtypeStruct((LANES, peers), F32),
            jax.ShapeDtypeStruct((8, LANES), F32),
        ),
        in_specs=[pl.BlockSpec(memory_space=pltpu.SMEM)] + whole(3),
        out_specs=tuple(whole(4)),
        name="places",
    )(me, counts, labels, ranks)


def pack_kernel(dest_ref, unit_ref, block_ref):
    rows = block_ref.shape[0]
    slots = iota((rows, dest_ref.shape[1]), 0) + pl.program_id(0) * rows
    pick = one_hot(dest_ref[...] == slots)
    block_ref[...] = jnp.dot(pick, unit_ref[...], preferred_element_type=F32).astype(BF16)


def packed(dest, unit, peers, cap):
    count, width = unit.shape
    rows = cap * 4
    return pl.pallas_call(
        pack_kernel,
        out_shape=jax.ShapeDtypeStruct((peers * cap, width), BF16),
        grid=(peers // 4,),
        in_specs=[pl.BlockSpec((1, count), lambda i: (0, 0)), pl.BlockSpec((count, width), lambda i: (0, 0))],
        out_specs=pl.BlockSpec((rows, width), lambda i: (i, 0)),
        compiler_params=pltpu.CompilerParams(vmem_limit_bytes=VMEM_LIMIT),
        name="pack",
    )(dest, unit)


def best_kernel(cap, ends_ref, ends_t_ref, rows_ref, best_ref):
    slots = rows_ref.shape[0]
    peers = ends_ref.shape[0]
    step = 512 if slots % 512 == 0 else 256

    def spread(place):
        sender = place // cap
        return sender, (place - sender * cap).astype(F32)

    sender, spot = spread(iota((peers, slots), 1))
    from_peer = jnp.where(sender == iota((peers, slots), 0), jnp.float32(1), jnp.float32(0))
    ends_row = jnp.dot(ends_t_ref[...], from_peer, precision=EXACT, preferred_element_type=F32)
    key_row = jnp.sum(jnp.where(ends_row <= spot[:1], 1.0, 0.0), axis=0, keepdims=True)
    sender, spot = spread(iota((slots, peers), 0))
    from_peer = jnp.where(sender == iota((slots, peers), 1), jnp.float32(1), jnp.float32(0))
    ends_col = jnp.dot(from_peer, ends_ref[...], precision=EXACT, preferred_element_type=F32)
    key_col = jnp.sum(jnp.where(ends_col <= spot[:, :1], 1.0, 0.0), axis=1, keepdims=True)

    for left in range(0, slots, step):
        columns = rows_ref[left : left + step, :]
        top = jnp.full((1, step), -1.0, F32)
        for upper in range(0, slots, step):
            gram = lax.dot_general(rows_ref[upper : upper + step, :], columns, NT, preferred_element_type=F32)
            keep = key_col[upper : upper + step] == key_row[:, left : left + step]
            if upper == left:
                keep = keep & (iota((step, step), 0) != iota((step, step), 1))
            top = jnp.maximum(top, jnp.max(jnp.where(keep, gram, -1.0), axis=0, keepdims=True))
        best_ref[:, left : left + step] = top


def bests(ends, ends_t, rows, cap):
    slots, width = rows.shape
    return pl.pallas_call(
        functools.partial(best_kernel, cap),
        out_shape=jax.ShapeDtypeStruct((1, slots), F32),
        in_specs=whole(3),
        out_specs=whole(1)[0],
        compiler_params=pltpu.CompilerParams(vmem_limit_bytes=VMEM_LIMIT),
        name="similar",
    )(ends, ends_t, rows)


def result_kernel(dest_ref, back_ref, out_ref):
    peers, cap = back_ref.shape
    back = back_ref[...]
    high = back.astype(BF16)
    rest = back - high.astype(F32)
    middle = rest.astype(BF16)
    low = (rest - middle.astype(F32)).astype(BF16)
    step = 512
    for at in range(0, dest_ref.shape[1], step):
        dest = dest_ref[:, at : at + step]
        owner = dest // cap
        hot = one_hot(dest - owner * cap == iota((cap, step), 0))
        parts = [jnp.dot(part, hot, preferred_element_type=F32) for part in (high, middle, low)]
        found = parts[0] + (parts[1] + parts[2])
        out_ref[:, at : at + step] = jnp.sum(jnp.where(owner == iota((peers, step), 0), found, 0.0), axis=0, keepdims=True)


def results(dest, back):
    return pl.pallas_call(
        result_kernel,
        out_shape=jax.ShapeDtypeStruct(dest.shape, F32),
        in_specs=whole(2),
        out_specs=whole(1)[0],
        name="results",
    )(dest, back)


def cluster_best(pair):
    blocks, flags = pair
    peers, owned, most, width = blocks.shape
    slots = peers * most
    members = jnp.transpose(blocks, (1, 0, 2, 3)).reshape(owned, slots, width)
    valid = jnp.transpose(flags, (1, 0, 2)).reshape(owned, slots) > 0.5
    off_diagonal = jnp.logical_not(jnp.eye(slots, dtype=bool))

    def one_cluster(item):
        rows_of, valid_of = item
        gram = jnp.dot(rows_of, rows_of.T, preferred_element_type=jnp.float32)
        keep = valid_of[None, :] & off_diagonal
        return jnp.max(jnp.where(keep, gram, jnp.float32(-1.0)), axis=1)

    best = lax.map(one_cluster, (members, valid))
    return jnp.transpose(best.reshape(owned, peers, most), (1, 0, 2))


def roomy(labels, ranks, unit):
    count, width = unit.shape
    peers = lax.axis_size("rows")
    owned = CLUSTERS // peers
    cluster_hot = (labels[:, None] == jnp.arange(CLUSTERS, dtype=I32)[None, :]).astype(F32)
    rank_hot = (ranks[:, None] == jnp.arange(MOST, dtype=I32)[None, :]).astype(F32)
    numbered = rank_hot * jnp.arange(1, count + 1, dtype=F32)[:, None]
    filled = jnp.dot(cluster_hot.T, rank_hot, precision=EXACT)
    member_idx = jnp.dot(cluster_hot.T, numbered, precision=EXACT).astype(I32) - 1
    member_idx = jnp.where(member_idx < 0, count, member_idx).reshape(CLUSTERS * MOST)
    padded = jnp.concatenate([unit, jnp.zeros((1, width), BF16)], axis=0)
    outgoing = padded[member_idx].reshape(peers, owned, MOST, width)
    occupied = filled.astype(BF16).reshape(peers, owned, MOST)
    best = cluster_best((exchange(outgoing), exchange(occupied)))
    table = exchange(best).reshape(CLUSTERS, MOST)
    per_row = jnp.dot(cluster_hot, table, precision=EXACT)
    return jnp.sum(per_row * rank_hot, axis=1)


def exchange(blocks):
    return lax.all_to_all(blocks, "rows", split_axis=0, concat_axis=0, tiled=True)


def local(embeddings, cluster_id):
    count, width = embeddings.shape
    peers = lax.axis_size("rows")
    cap = -(-(count // peers + SLACK) // 16) * 16
    labels = cluster_id.reshape(1, count)
    ranks, counts = ranks_and_counts(labels, peers)
    counts = exchange(counts.reshape(peers, 1, CLUSTERS)).reshape(peers, CLUSTERS)
    unit = unit_rows(embeddings)
    me = lax.axis_index("rows").reshape(1)
    dest, ends, ends_t, most = places(me, counts, labels, ranks, cap)
    arrived = exchange(packed(dest, unit, peers, cap).reshape(peers, cap, width))
    best = bests(ends, ends_t, arrived.reshape(peers * cap, width), cap)
    back = exchange(best.reshape(peers, 1, cap)).reshape(peers, cap)
    nearest = results(dest, back).reshape(count)
    return lax.cond(
        most[0, 0] > cap,
        lambda labels, ranks, unit, nearest: roomy(labels.reshape(count), ranks.reshape(count), unit),
        lambda labels, ranks, unit, nearest: nearest,
        labels, ranks, unit, nearest,
    )


def solution(mesh):
    return jax.shard_map(
        local,
        mesh=mesh,
        in_specs=(P(("groups", "rows"), None), P(("groups", "rows"), None)),
        out_specs=P(("groups", "rows")),
        check_vma=False,
    )
```

```python
import functools

import jax
import jax.numpy as jnp
from jax import lax
from jax.experimental import pallas as pl
from jax.experimental.pallas import tpu as pltpu
from jax.sharding import PartitionSpec as P

CLUSTERS = 512
MOST = 16
LANES = 128
SLACK = 16
ROUNDS = 8
EXACT = lax.Precision.HIGHEST
BF16, F32, I32 = jnp.bfloat16, jnp.float32, jnp.int32
VMEM_LIMIT = 48 * 1024 * 1024
NT = (((1,), (1,)), ((), ()))


def iota(shape, dim):
    return lax.broadcasted_iota(I32, shape, dim)


def one_hot(mask):
    return jnp.where(mask, jnp.float32(1), jnp.float32(0)).astype(BF16)


def whole(count):
    return [pl.BlockSpec(memory_space=pltpu.VMEM)] * count


def count_kernel(label_ref, count_ref):
    step = 512
    ones = jnp.ones((count_ref.shape[0], step), BF16)
    counts = jnp.zeros((count_ref.shape[0], CLUSTERS), F32)
    for at in range(0, label_ref.shape[1], step):
        hot = one_hot(label_ref[:, at : at + step] == iota((CLUSTERS, step), 0))
        counts = counts + lax.dot_general(ones, hot, NT, preferred_element_type=F32)
    count_ref[:, 0, :] = counts


def counted(labels, peers):
    return pl.pallas_call(
        count_kernel,
        out_shape=jax.ShapeDtypeStruct((peers, 1, CLUSTERS), F32),
        in_specs=whole(1),
        out_specs=whole(1)[0],
        name="counts",
    )(labels)


def rank_kernel(label_ref, rank_ref):
    step = 256
    tri = one_hot((iota((step, step + LANES), 0) < iota((step, step + LANES), 1)) | (iota((step, step + LANES), 1) >= step))
    running = jnp.zeros((CLUSTERS, LANES), F32)
    for at in range(0, label_ref.shape[1], step):
        hot = label_ref[:, at : at + step] == iota((CLUSTERS, step), 0)
        before = jnp.dot(one_hot(hot), tri, preferred_element_type=F32)
        here = before[:, :step] + jnp.concatenate([running] * (step // LANES), axis=1)
        rank_ref[:, at : at + step] = jnp.sum(jnp.where(hot, here, 0.0), axis=0, keepdims=True).astype(I32)
        running = running + before[:, step:]


def ranked(labels):
    return pl.pallas_call(
        rank_kernel,
        out_shape=jax.ShapeDtypeStruct(labels.shape, I32),
        in_specs=whole(1),
        out_specs=whole(1)[0],
        cost_estimate=pl.CostEstimate(flops=labels.shape[1] * CLUSTERS * 8, bytes_accessed=1 << 22, transcendentals=0),
        name="ranks",
    )(labels)


def unit_kernel(rows_ref, unit_ref):
    values = rows_ref[...].astype(F32)
    total = jnp.sum(values * values, axis=1, keepdims=True)
    unit_ref[...] = (values * lax.rsqrt(total + 1e-06)).astype(BF16)


def unit_rows(embeddings):
    count, width = embeddings.shape
    step = min(512, count)
    spec = pl.BlockSpec((step, width), lambda i: (i, 0))
    return pl.pallas_call(
        unit_kernel,
        out_shape=jax.ShapeDtypeStruct((count, width), BF16),
        grid=(count // step,),
        in_specs=[spec],
        out_specs=spec,
        cost_estimate=pl.CostEstimate(flops=4 * count * width, bytes_accessed=4 * count * width, transcendentals=count),
        name="unit",
    )(embeddings)


def swapped_evenly(table, peers):
    pieces = [table[:, at : at + LANES] for at in range(0, CLUSTERS, LANES)]
    lane = iota((1, LANES), 1)

    def over_laps(parts, combine):
        found = functools.reduce(combine, parts)
        shift = peers
        while shift < LANES:
            found = combine(found, pltpu.roll(found, shift, 1))
            shift *= 2
        return found

    bits = [1 << i for i in range(peers.bit_length() - 1)]
    for bit in (bits * ROUNDS)[:ROUNDS]:

        def partner(x):
            return jnp.where((lane & bit) == 0, pltpu.roll(x, LANES - bit, 1), pltpu.roll(x, bit, 1))

        load = over_laps([piece[:peers] for piece in pieces], jnp.add)
        excess = load - partner(load)
        others = [partner(piece) for piece in pieces]
        gains = []
        for piece, other in zip(pieces, others):
            moved = piece[:peers] - other[:peers]
            gains.append(jnp.sum(moved * (excess - moved), axis=0, keepdims=True))
        best = over_laps(gains, jnp.maximum)
        pieces = [
            jnp.where((gain == best) & (gain > 0.0), other, piece) for gain, other, piece in zip(gains, others, pieces)
        ]
    return jnp.concatenate(pieces, axis=1)


def place_kernel(cap, me_ref, count_ref, label_ref, rank_ref, dest_ref, ends_ref, ends_t_ref, most_ref):
    me = me_ref[0]
    counts = count_ref[:, 0, :]
    peers = counts.shape[0]
    square = (CLUSTERS, CLUSTERS)
    total = jnp.sum(counts, axis=0, keepdims=True)
    total_col = jnp.transpose(jnp.broadcast_to(total, (LANES, CLUSTERS)))[:, :1]
    first, second = iota(square, 0), iota(square, 1)
    ahead = (total_col > total) | ((total_col == total) & (first < second))
    turn = (CLUSTERS - 1) - jnp.sum(jnp.where(ahead, 1.0, 0.0), axis=1, keepdims=True).astype(I32)
    lap = turn // peers
    spot = turn - lap * peers
    place = lap * peers + jnp.where(lap % 2 == 0, spot, peers - 1 - spot)
    number = iota((8, CLUSTERS), 1)
    digits = jnp.where(iota((8, CLUSTERS), 0) == 0, number // MOST, number % MOST).astype(F32)
    table = jnp.concatenate([counts, digits], axis=0).astype(BF16)
    table = jnp.dot(table, one_hot(place == second), preferred_element_type=F32)
    table = swapped_evenly(table, peers)

    counts = table[:peers]
    cluster = table[peers : peers + 1] * MOST + table[peers + 1 : peers + 2]
    cluster_col = jnp.transpose(jnp.broadcast_to(cluster, (LANES, CLUSTERS)))[:, :1].astype(I32)
    earlier = one_hot((first % peers == second % peers) & (first // peers < second // peers))
    offset = jnp.dot(counts.astype(BF16), earlier, preferred_element_type=F32)
    ends = offset + counts
    most_ref[...] = jnp.broadcast_to(jnp.max(ends, axis=(0, 1), keepdims=True), most_ref.shape)

    mine = jnp.sum(jnp.where(iota(counts.shape, 0) == me, offset, 0.0), axis=0, keepdims=True).astype(I32)
    upper = mine // MOST
    lane = iota((1, CLUSTERS), 1)
    find = jnp.concatenate([lane % peers, upper, mine - upper * MOST] + [jnp.zeros_like(mine)] * 5, axis=0)
    find = find.astype(F32).astype(BF16)
    step = 512
    for at in range(0, label_ref.shape[1], step):
        hot = one_hot(label_ref[:, at : at + step] == cluster_col)
        found = jnp.dot(find, hot, preferred_element_type=F32).astype(I32)
        slot = found[1:2] * MOST + found[2:3] + rank_ref[:, at : at + step]
        dest_ref[:, at : at + step] = jnp.where(slot < cap, found[0:1] * cap + slot, -1)

    chosen = lane == iota((LANES, CLUSTERS), 0) * peers + me
    chosen = jnp.where(chosen, jnp.float32(1), jnp.float32(0))
    never = jnp.float32(1 << 20)
    owned = CLUSTERS // peers
    own = lax.dot_general(ends, chosen, NT, precision=EXACT, preferred_element_type=F32)
    ends_ref[...] = jnp.where(iota(own.shape, 1) < owned, own, never)
    own_t = lax.dot_general(chosen, ends, NT, precision=EXACT, preferred_element_type=F32)
    ends_t_ref[...] = jnp.where(iota(own_t.shape, 0) < owned, own_t, never)


def places(me, counts, labels, ranks, cap):
    peers = counts.shape[0]
    return pl.pallas_call(
        functools.partial(place_kernel, cap),
        out_shape=(
            jax.ShapeDtypeStruct(labels.shape, I32),
            jax.ShapeDtypeStruct((peers, LANES), F32),
            jax.ShapeDtypeStruct((LANES, peers), F32),
            jax.ShapeDtypeStruct((8, LANES), F32),
        ),
        in_specs=[pl.BlockSpec(memory_space=pltpu.SMEM)] + whole(3),
        out_specs=tuple(whole(4)),
        name="places",
    )(me, counts, labels, ranks)


def pack_kernel(dest_ref, unit_ref, block_ref):
    rows = block_ref.shape[0]
    slots = iota((rows, dest_ref.shape[1]), 0) + pl.program_id(0) * rows
    pick = one_hot(dest_ref[...] == slots)
    block_ref[...] = jnp.dot(pick, unit_ref[...], preferred_element_type=F32).astype(BF16)


def packed(dest, unit, peers, cap):
    count, width = unit.shape
    rows = cap * 4
    return pl.pallas_call(
        pack_kernel,
        out_shape=jax.ShapeDtypeStruct((peers * cap, width), BF16),
        grid=(peers // 4,),
        in_specs=[pl.BlockSpec((1, count), lambda i: (0, 0)), pl.BlockSpec((count, width), lambda i: (0, 0))],
        out_specs=pl.BlockSpec((rows, width), lambda i: (i, 0)),
        compiler_params=pltpu.CompilerParams(vmem_limit_bytes=VMEM_LIMIT),
        name="pack",
    )(dest, unit)


def chunk_depth(peers, cap):
    return max(deep for deep in range(16, cap + 1, 16) if cap % deep == 0 and (deep == 16 or deep * peers <= 1024))


def key_kernel(cap, deep, ends_ref, ends_t_ref, row_ref, col_ref, meet_ref):
    peers = ends_ref.shape[0]
    owned = CLUSTERS // peers
    size = peers * deep
    chunks = cap // deep
    slots = peers * cap

    def spread(shape, dim):
        index = iota(shape, dim)
        chunk = index // size
        within = index - chunk * size
        sender = within // deep
        return sender, (chunk * deep + within - sender * deep).astype(F32)

    sender, spot = spread((peers, slots), 1)
    from_peer = jnp.where(sender == iota((peers, slots), 0), jnp.float32(1), jnp.float32(0))
    ends = jnp.dot(ends_t_ref[...], from_peer, precision=EXACT, preferred_element_type=F32)
    row = jnp.sum(jnp.where(ends <= spot[:1], 1.0, 0.0), axis=0, keepdims=True)
    sender, spot = spread((slots, peers), 0)
    from_peer = jnp.where(sender == iota((slots, peers), 1), jnp.float32(1), jnp.float32(0))
    ends = jnp.dot(from_peer, ends_ref[...], precision=EXACT, preferred_element_type=F32)
    col = jnp.sum(jnp.where(ends <= spot[:, :1], 1.0, 0.0), axis=1, keepdims=True)
    lows, highs = [], []
    for chunk in range(chunks):
        part = row[:, chunk * size : (chunk + 1) * size]
        row_ref[chunk] = part
        col_ref[chunk] = col[chunk * size : (chunk + 1) * size]
        lows.append(jnp.min(part))
        highs.append(jnp.max(jnp.where(part < owned, part, -1.0)))
    for left in range(chunks):
        for right in range(left, chunks):
            overlap = (lows[left] <= highs[right]) & (lows[right] <= highs[left])
            meet_ref[left * chunks + right] = jnp.where(overlap, 1, 0)


def keys(ends, ends_t, cap, deep):
    peers = ends.shape[0]
    chunks, size = cap // deep, peers * deep
    return pl.pallas_call(
        functools.partial(key_kernel, cap, deep),
        out_shape=(
            jax.ShapeDtypeStruct((chunks, 1, size), F32),
            jax.ShapeDtypeStruct((chunks, size, 1), F32),
            jax.ShapeDtypeStruct((chunks * chunks,), I32),
        ),
        in_specs=whole(2),
        out_specs=tuple(whole(2) + [pl.BlockSpec(memory_space=pltpu.SMEM)]),
        cost_estimate=pl.CostEstimate(flops=1 << 28, bytes_accessed=1 << 22, transcendentals=0),
        compiler_params=pltpu.CompilerParams(vmem_limit_bytes=VMEM_LIMIT),
        name="keys",
    )(ends, ends_t)


def best_kernel(deep, meet_ref, row_ref, col_ref, rows_ref, best_ref, held, top, side, arrived):
    peers, cap, width = rows_ref.shape
    chunks, size = held.shape[0], peers * deep
    step = 256
    copies = []
    for chunk in range(chunks):
        copy = pltpu.make_async_copy(rows_ref.at[:, pl.ds(chunk * deep, deep), :], held.at[chunk], arrived.at[chunk])
        copy.start()
        copies.append(copy)
    top[...] = jnp.full(top.shape, -1.0, F32)
    side[...] = jnp.full(side.shape, -1.0, F32)
    for right in range(chunks):
        copies[right].wait()

        def with_left(left, carry):
            @pl.when(meet_ref[left * chunks + right] == 1)
            def _():
                upper = held[left].reshape(size, width)
                key_col = col_ref[left]
                for at in range(0, size, step):
                    lower = held[right].reshape(size, width)[at : at + step]
                    gram = lax.dot_general(upper, lower, NT, preferred_element_type=F32)
                    keep = key_col == row_ref[right, :, at : at + step]
                    same = iota((size, step), 0) - iota((size, step), 1) == jnp.where(left == right, at, -size)
                    gram = jnp.where(keep & jnp.logical_not(same), gram, -1.0)
                    top[right, :, at : at + step] = jnp.maximum(
                        top[right, :, at : at + step], jnp.max(gram, axis=0, keepdims=True)
                    )
                    halves = [gram[:, i : i + LANES] for i in range(0, step, LANES)]
                    side[left] = functools.reduce(jnp.maximum, halves, side[left])

            return carry

        lax.fori_loop(0, right + 1, with_left, 0)
    for chunk in range(chunks):
        found = jnp.maximum(top[chunk], jnp.max(jnp.transpose(side[chunk]), axis=0, keepdims=True))
        for sender in range(peers):
            best_ref[sender, :, chunk * deep : (chunk + 1) * deep] = found[:, sender * deep : (sender + 1) * deep]


def bests(meet, key_row, key_col, rows, deep):
    peers, cap, width = rows.shape
    chunks, size = cap // deep, peers * deep
    return pl.pallas_call(
        functools.partial(best_kernel, deep),
        out_shape=jax.ShapeDtypeStruct((peers, 1, cap), F32),
        in_specs=[pl.BlockSpec(memory_space=pltpu.SMEM)] + whole(2) + [pl.BlockSpec(memory_space=pl.ANY)],
        out_specs=whole(1)[0],
        scratch_shapes=[
            pltpu.VMEM((chunks, peers, deep, width), BF16),
            pltpu.VMEM((chunks, 1, size), F32),
            pltpu.VMEM((chunks, size, LANES), F32),
            pltpu.SemaphoreType.DMA((chunks,)),
        ],
        compiler_params=pltpu.CompilerParams(vmem_limit_bytes=VMEM_LIMIT),
        name="similar",
    )(meet, key_row, key_col, rows)


def result_kernel(dest_ref, back_ref, out_ref):
    peers, _, cap = back_ref.shape
    back = back_ref[:, 0, :]
    high = back.astype(BF16)
    rest = back - high.astype(F32)
    middle = rest.astype(BF16)
    low = (rest - middle.astype(F32)).astype(BF16)
    step = 512
    for at in range(0, dest_ref.shape[1], step):
        dest = dest_ref[:, at : at + step]
        owner = dest // cap
        hot = one_hot(dest - owner * cap == iota((cap, step), 0))
        parts = [jnp.dot(part, hot, preferred_element_type=F32) for part in (high, middle, low)]
        found = parts[0] + (parts[1] + parts[2])
        out_ref[:, at : at + step] = jnp.sum(jnp.where(owner == iota((peers, step), 0), found, 0.0), axis=0, keepdims=True)


def results(dest, back):
    return pl.pallas_call(
        result_kernel,
        out_shape=jax.ShapeDtypeStruct(dest.shape, F32),
        in_specs=whole(2),
        out_specs=whole(1)[0],
        name="results",
    )(dest, back)


def cluster_best(pair):
    blocks, flags = pair
    peers, owned, most, width = blocks.shape
    slots = peers * most
    members = jnp.transpose(blocks, (1, 0, 2, 3)).reshape(owned, slots, width)
    valid = jnp.transpose(flags, (1, 0, 2)).reshape(owned, slots) > 0.5
    off_diagonal = jnp.logical_not(jnp.eye(slots, dtype=bool))

    def one_cluster(item):
        rows_of, valid_of = item
        gram = jnp.dot(rows_of, rows_of.T, preferred_element_type=jnp.float32)
        keep = valid_of[None, :] & off_diagonal
        return jnp.max(jnp.where(keep, gram, jnp.float32(-1.0)), axis=1)

    best = lax.map(one_cluster, (members, valid))
    return jnp.transpose(best.reshape(owned, peers, most), (1, 0, 2))


def roomy(labels, ranks, unit):
    count, width = unit.shape
    peers = lax.axis_size("rows")
    owned = CLUSTERS // peers
    cluster_hot = (labels[:, None] == jnp.arange(CLUSTERS, dtype=I32)[None, :]).astype(F32)
    rank_hot = (ranks[:, None] == jnp.arange(MOST, dtype=I32)[None, :]).astype(F32)
    numbered = rank_hot * jnp.arange(1, count + 1, dtype=F32)[:, None]
    filled = jnp.dot(cluster_hot.T, rank_hot, precision=EXACT)
    member_idx = jnp.dot(cluster_hot.T, numbered, precision=EXACT).astype(I32) - 1
    member_idx = jnp.where(member_idx < 0, count, member_idx).reshape(CLUSTERS * MOST)
    padded = jnp.concatenate([unit, jnp.zeros((1, width), BF16)], axis=0)
    outgoing = padded[member_idx].reshape(peers, owned, MOST, width)
    occupied = filled.astype(BF16).reshape(peers, owned, MOST)
    best = cluster_best((exchange(outgoing), exchange(occupied)))
    table = exchange(best).reshape(CLUSTERS, MOST)
    per_row = jnp.dot(cluster_hot, table, precision=EXACT)
    return jnp.sum(per_row * rank_hot, axis=1)


def exchange(blocks):
    return lax.all_to_all(blocks, "rows", split_axis=0, concat_axis=0, tiled=True)


def local(embeddings, cluster_id):
    count, width = embeddings.shape
    peers = lax.axis_size("rows")
    cap = -(-(count // peers + SLACK) // 16) * 16
    deep = chunk_depth(peers, cap)
    labels = cluster_id.reshape(1, count)
    counts = exchange(counted(labels, peers))
    ranks = ranked(labels)
    unit = unit_rows(embeddings)
    me = lax.axis_index("rows").reshape(1)
    dest, ends, ends_t, most = places(me, counts, labels, ranks, cap)
    arrived = exchange(packed(dest, unit, peers, cap).reshape(peers, cap, width))
    key_row, key_col, meet = keys(ends, ends_t, cap, deep)
    back = exchange(bests(meet, key_row, key_col, arrived, deep))
    nearest = results(dest, back).reshape(count)
    return lax.cond(
        most[0, 0] > cap,
        lambda labels, ranks, unit, nearest: roomy(labels.reshape(count), ranks.reshape(count), unit),
        lambda labels, ranks, unit, nearest: nearest,
        labels, ranks, unit, nearest,
    )


def solution(mesh):
    return jax.shard_map(
        local,
        mesh=mesh,
        in_specs=(P(("groups", "rows"), None), P(("groups", "rows"), None)),
        out_specs=P(("groups", "rows")),
        check_vma=False,
    )
```

```python
import functools

import jax
import jax.numpy as jnp
import numpy as np
from jax import lax
from jax.experimental import pallas as pl
from jax.experimental.pallas import tpu as pltpu
from jax.sharding import PartitionSpec as P

CLUSTERS = 512
MOST = 16
LANES = 128
SLACK = 16
ROUNDS = 6
EARLY = 3
LATE = 3
EXACT = lax.Precision.HIGHEST
BF16, F32, I32 = jnp.bfloat16, jnp.float32, jnp.int32
VMEM_LIMIT = 24 * 1024 * 1024
SMALL_VMEM = 12 * 1024 * 1024
NT = (((1,), (1,)), ((), ()))


def iota(shape, dim):
    return lax.broadcasted_iota(I32, shape, dim)


def one_hot(mask):
    return jnp.where(mask, jnp.float32(1), jnp.float32(0)).astype(BF16)


def quotient(index, by, limit):
    numbers = np.arange(limit)
    for shift in range(8, 24):
        factor = -(-(1 << shift) // by)
        if limit * factor < 1 << 31 and np.array_equal(numbers * factor >> shift, numbers // by):
            return (index * factor) >> shift
    raise ValueError("no factor")


def whole(count):
    return [pl.BlockSpec(memory_space=pltpu.VMEM)] * count


def count_kernel(label_ref, count_ref):
    step = 512
    ones = jnp.ones((count_ref.shape[0], step), BF16)
    counts = jnp.zeros((count_ref.shape[0], CLUSTERS), F32)
    for at in range(0, label_ref.shape[1], step):
        hot = one_hot(label_ref[:, at : at + step] == iota((CLUSTERS, step), 0))
        counts = counts + lax.dot_general(ones, hot, NT, preferred_element_type=F32)
    count_ref[:, 0, :] = counts


def counted(labels, peers):
    return pl.pallas_call(
        count_kernel,
        out_shape=jax.ShapeDtypeStruct((peers, 1, CLUSTERS), F32),
        in_specs=whole(1),
        out_specs=whole(1)[0],
        compiler_params=pltpu.CompilerParams(vmem_limit_bytes=SMALL_VMEM),
        name="counts",
    )(labels)


def rank_kernel(label_ref, rank_ref):
    step = 256
    tri = one_hot((iota((step, step + LANES), 0) < iota((step, step + LANES), 1)) | (iota((step, step + LANES), 1) >= step))
    running = jnp.zeros((CLUSTERS, LANES), F32)
    for at in range(0, label_ref.shape[1], step):
        hot = label_ref[:, at : at + step] == iota((CLUSTERS, step), 0)
        before = jnp.dot(one_hot(hot), tri, preferred_element_type=F32)
        here = before[:, :step] + jnp.concatenate([running] * (step // LANES), axis=1)
        rank_ref[:, at : at + step] = jnp.sum(jnp.where(hot, here, 0.0), axis=0, keepdims=True).astype(I32)
        running = running + before[:, step:]


def ranked(labels):
    return pl.pallas_call(
        rank_kernel,
        out_shape=jax.ShapeDtypeStruct(labels.shape, I32),
        in_specs=whole(1),
        out_specs=whole(1)[0],
        cost_estimate=pl.CostEstimate(flops=labels.shape[1] * CLUSTERS * 8, bytes_accessed=1 << 22, transcendentals=0),
        compiler_params=pltpu.CompilerParams(vmem_limit_bytes=SMALL_VMEM),
        name="ranks",
    )(labels)


def unit_kernel(rows_ref, unit_ref):
    values = rows_ref[...].astype(F32)
    total = jnp.sum(values * values, axis=1, keepdims=True)
    unit_ref[...] = (values * lax.rsqrt(total + 1e-06)).astype(BF16)


def unit_rows(embeddings):
    count, width = embeddings.shape
    step = min(512, count)
    spec = pl.BlockSpec((step, width), lambda i: (i, 0))
    return pl.pallas_call(
        unit_kernel,
        out_shape=jax.ShapeDtypeStruct((count, width), BF16),
        grid=(count // step,),
        in_specs=[spec],
        out_specs=spec,
        cost_estimate=pl.CostEstimate(flops=4 * count * width, bytes_accessed=4 * count * width, transcendentals=count),
        compiler_params=pltpu.CompilerParams(vmem_limit_bytes=SMALL_VMEM),
        name="unit",
    )(embeddings)


def swapped_evenly(table, peers):
    pieces = [table[:, at : at + LANES] for at in range(0, CLUSTERS, LANES)]
    lane = iota((1, LANES), 1)

    def over_laps(parts, combine):
        found = functools.reduce(combine, parts)
        shift = peers
        while shift < LANES:
            found = combine(found, pltpu.roll(found, shift, 1))
            shift *= 2
        return found

    bits = [1 << i for i in range(peers.bit_length() - 1)]
    for bit in (bits * ROUNDS)[:ROUNDS]:

        def partner(x):
            return jnp.where((lane & bit) == 0, pltpu.roll(x, LANES - bit, 1), pltpu.roll(x, bit, 1))

        load = over_laps([piece[:peers] for piece in pieces], jnp.add)
        excess = load - partner(load)
        others = [partner(piece) for piece in pieces]
        gains = []
        for piece, other in zip(pieces, others):
            moved = piece[:peers] - other[:peers]
            gains.append(jnp.sum(moved * (excess - moved), axis=0, keepdims=True))
        best = over_laps(gains, jnp.maximum)
        pieces = [
            jnp.where((gain == best) & (gain > 0.0), other, piece) for gain, other, piece in zip(gains, others, pieces)
        ]
    return jnp.concatenate(pieces, axis=1)


def offsets(table, peers):
    square = (CLUSTERS, CLUSTERS)
    bits = peers.bit_length() - 1
    first, second = iota(square, 0), iota(square, 1)
    earlier = one_hot((((first ^ second) & (peers - 1)) == 0) & ((first >> bits) < (second >> bits)))
    return jnp.dot(table[:peers].astype(BF16), earlier, preferred_element_type=F32)


def place_kernel(cap, me_ref, count_ref, label_ref, rank_ref, dest_ref, table_ref):
    me = me_ref[0]
    counts = count_ref[:, 0, :]
    peers = counts.shape[0]
    bits = peers.bit_length() - 1
    square = (CLUSTERS, CLUSTERS)
    total = jnp.sum(counts, axis=0, keepdims=True)
    total_col = jnp.transpose(jnp.broadcast_to(total, (LANES, CLUSTERS)))[:, :1]
    first, second = iota(square, 0), iota(square, 1)
    ahead = (total_col > total) | ((total_col == total) & (first < second))
    turn = (CLUSTERS - 1) - jnp.sum(jnp.where(ahead, 1.0, 0.0), axis=1, keepdims=True).astype(I32)
    place = jnp.where(((turn >> bits) & 1) == 0, turn, turn ^ (peers - 1))
    number = iota((8, CLUSTERS), 1)
    digits = jnp.where(iota((8, CLUSTERS), 0) == 0, number >> 4, number & 15).astype(F32)
    table = jnp.concatenate([counts, digits], axis=0).astype(BF16)
    table = jnp.dot(table, one_hot(place == second), preferred_element_type=F32)
    table = swapped_evenly(table, peers)
    table_ref[...] = table

    offset = offsets(table, peers)
    mine = jnp.sum(jnp.where(iota(counts.shape, 0) == me, offset, 0.0), axis=0, keepdims=True)
    base = mine + ((iota((1, CLUSTERS), 1) & (peers - 1)) * cap).astype(F32)
    cluster = table[peers : peers + 1] * 16.0 + table[peers + 1 : peers + 2]
    both = jnp.transpose(jnp.where(iota((LANES, CLUSTERS), 0) == 0, cluster, base))
    cluster_col, base_col = both[:, :1].astype(I32), both[:, 1:2]
    step = 512
    for at in range(0, label_ref.shape[1], step):
        hot = label_ref[:, at : at + step] == cluster_col
        slot = jnp.sum(jnp.where(hot, base_col, 0.0), axis=0, keepdims=True).astype(I32)
        dest_ref[:, at : at + step] = slot + rank_ref[:, at : at + step]


def places(me, counts, labels, ranks, cap):
    peers = counts.shape[0]
    return pl.pallas_call(
        functools.partial(place_kernel, cap),
        out_shape=(jax.ShapeDtypeStruct(labels.shape, I32), jax.ShapeDtypeStruct((peers + 8, CLUSTERS), F32)),
        in_specs=[pl.BlockSpec(memory_space=pltpu.SMEM)] + whole(3),
        out_specs=tuple(whole(2)),
        compiler_params=pltpu.CompilerParams(vmem_limit_bytes=SMALL_VMEM),
        name="places",
    )(me, counts, labels, ranks)


def sender_of(me, block, peers):
    half = peers // 2
    return jnp.where(block < half, (me & -half) + block, me ^ block)


def pack_kernel(cap, peers, numbers, me_ref, dest_ref, unit_ref, *block_refs):
    me = me_ref[0]
    count = dest_ref.shape[1]
    per_ref = block_refs[0].shape[0] // cap
    group = 4
    for at in range(0, len(numbers), group):
        some = numbers[at : at + group]
        index = iota((len(some) * cap, 1), 0)
        slots = index
        for i, number in enumerate(some):
            shift = (sender_of(me, number, peers) - i) * cap
            slots = jnp.where((index >= i * cap) & (index < (i + 1) * cap), index + shift, slots)
        pick = one_hot(dest_ref[...] == slots)
        rows = jnp.dot(pick, unit_ref[...], preferred_element_type=F32).astype(BF16)
        for i in range(len(some)):
            block, within = divmod(at + i, per_ref)
            block_refs[block][within * cap : (within + 1) * cap, :] = rows[i * cap : (i + 1) * cap]


def packed(me, dest, unit, cap, peers, numbers, per_block=1):
    count, width = unit.shape
    rows = len(numbers) * cap
    blocks = len(numbers) // per_block
    return pl.pallas_call(
        functools.partial(pack_kernel, cap, peers, numbers),
        out_shape=tuple([jax.ShapeDtypeStruct((per_block * cap, width), BF16)] * blocks),
        in_specs=[pl.BlockSpec(memory_space=pltpu.SMEM)] + whole(2),
        out_specs=tuple(whole(blocks)),
        cost_estimate=pl.CostEstimate(
            flops=2 * rows * count * width, bytes_accessed=2 * width * (count + rows), transcendentals=0
        ),
        compiler_params=pltpu.CompilerParams(vmem_limit_bytes=VMEM_LIMIT),
        name="pack",
    )(me, dest, unit)


def key_kernel(cap, me_ref, table_ref, row_ref, col_ref, most_ref):
    me = me_ref[0]
    peers = table_ref.shape[0] - 8
    bits = peers.bit_length() - 1
    owned = CLUSTERS // peers
    slots = peers * cap
    ends = offsets(table_ref[...], peers) + table_ref[:peers]
    most_ref[...] = jnp.broadcast_to(jnp.max(ends, axis=(0, 1), keepdims=True), most_ref.shape)
    chosen = iota((LANES, CLUSTERS), 1) == (iota((LANES, CLUSTERS), 0) << bits) + me
    chosen = jnp.where(chosen, jnp.float32(1), jnp.float32(0))
    own = lax.dot_general(chosen, ends, NT, precision=EXACT, preferred_element_type=F32)
    own = jnp.where(iota(own.shape, 0) < owned, own, jnp.float32(1 << 20))

    index = iota((1, slots), 1)
    block = quotient(index, cap, slots)
    spot = (index - block * cap).astype(F32)
    from_peer = sender_of(me, block, peers) == iota((peers, slots), 0)
    from_peer = jnp.where(from_peer, jnp.float32(1), jnp.float32(0))
    ends = jnp.dot(own, from_peer, precision=EXACT, preferred_element_type=F32)
    row = jnp.sum(jnp.where(ends <= spot, 1.0, 0.0), axis=0, keepdims=True)
    row_ref[...] = row
    col_ref[...] = jnp.transpose(jnp.broadcast_to(row, (LANES, slots)))


def keys(me, table, cap):
    peers = table.shape[0] - 8
    slots = peers * cap
    return pl.pallas_call(
        functools.partial(key_kernel, cap),
        out_shape=(
            jax.ShapeDtypeStruct((1, slots), F32),
            jax.ShapeDtypeStruct((slots, LANES), F32),
            jax.ShapeDtypeStruct((8, LANES), F32),
        ),
        in_specs=[pl.BlockSpec(memory_space=pltpu.SMEM)] + whole(1),
        out_specs=tuple(whole(3)),
        cost_estimate=pl.CostEstimate(flops=1 << 28, bytes_accessed=1 << 22, transcendentals=0),
        compiler_params=pltpu.CompilerParams(vmem_limit_bytes=SMALL_VMEM),
        name="keys",
    )(me, table)


def rows_of(refs, cap, start, count):
    found, at = [], 0
    for ref in refs:
        blocks = ref.shape[0] // cap
        low, high = max(start, at), min(start + count, at + blocks)
        if low < high:
            found.append(ref[(low - at) * cap : (high - at) * cap, :])
        at += blocks
    return found[0] if len(found) == 1 else jnp.concatenate(found, axis=0)


def masked_parts(rows, columns, key_col, key_row, itself):
    gram = lax.dot_general(rows, columns, NT, preferred_element_type=F32)
    height, width = gram.shape
    parts = []
    for lane in range(0, width, LANES):
        wide = min(LANES, width - lane)
        part = gram[:, lane : lane + wide]
        keep = key_col[:, :wide] == key_row[:, lane : lane + wide]
        if -width < itself < height:
            keep = keep & (iota(part.shape, 0) - iota(part.shape, 1) != itself + lane)
        parts.append(jnp.where(keep, part, -1.0))
    return parts


def largest(parts):
    return jnp.concatenate([jnp.max(part, axis=0, keepdims=True) for part in parts], axis=1)


def first_kernel(cap, known, row_ref, col_ref, *refs):
    *block_refs, best_ref = refs
    tall, broad = max(1, 576 // cap), max(1, 432 // cap)
    for left in range(0, known, broad):
        count = min(broad, known - left)
        columns = rows_of(block_refs, cap, left, count)
        key_row = row_ref[:, left * cap : (left + count) * cap]
        best = jnp.full((1, count * cap), -1.0, F32)
        for upper in range(0, known, tall):
            rows = rows_of(block_refs, cap, upper, min(tall, known - upper))
            key_col = col_ref[upper * cap : upper * cap + rows.shape[0], :]
            best = jnp.maximum(best, largest(masked_parts(rows, columns, key_col, key_row, (left - upper) * cap)))
        for i in range(count):
            best_ref[left + i] = best[:, i * cap : (i + 1) * cap]


def last_kernel(cap, known, me_ref, row_ref, col_ref, before_ref, *refs):
    *block_refs, best_ref = refs
    me = me_ref[0]
    peers = best_ref.shape[0]
    tall = max(1, 576 // cap)
    columns = rows_of(block_refs, cap, known, peers - known)
    key_row = row_ref[:, known * cap :]
    best = jnp.full((1, (peers - known) * cap), -1.0, F32)
    for upper in range(0, peers, tall):
        count = min(tall, peers - upper)
        rows = rows_of(block_refs, cap, upper, count)
        key_col = col_ref[upper * cap : (upper + count) * cap, :]
        parts = masked_parts(rows, columns, key_col, key_row, (known - upper) * cap)
        best = jnp.maximum(best, largest(parts))
        if upper < known:
            tail = parts[-1]
            if tail.shape[1] < LANES:
                tail = jnp.concatenate([tail, jnp.full((count * cap, LANES - tail.shape[1]), -1.0, F32)], axis=1)
            side = functools.reduce(jnp.maximum, parts[:-1] + [tail])
            for i in range(min(count, known - upper)):
                across = jnp.max(jnp.transpose(side[i * cap : (i + 1) * cap]), axis=0, keepdims=True)
                best_ref[sender_of(me, upper + i, peers)] = jnp.maximum(before_ref[upper + i], across)
    for i in range(peers - known):
        best_ref[sender_of(me, known + i, peers)] = best[:, i * cap : (i + 1) * cap]


def call_bests(kernel, scalars, arrays, blocks, out_blocks, fresh, cap):
    rows = sum(block.shape[0] for block in blocks)
    return pl.pallas_call(
        kernel,
        out_shape=jax.ShapeDtypeStruct((out_blocks, 1, cap), F32),
        in_specs=[pl.BlockSpec(memory_space=pltpu.SMEM)] * len(scalars) + whole(len(arrays) + len(blocks)),
        out_specs=whole(1)[0],
        cost_estimate=pl.CostEstimate(
            flops=2 * fresh * cap * rows * blocks[0].shape[1], bytes_accessed=1 << 23, transcendentals=0
        ),
        compiler_params=pltpu.CompilerParams(vmem_limit_bytes=VMEM_LIMIT),
        name="similar",
    )(*scalars, *arrays, *blocks)


def three_parts(values):
    high = values.astype(BF16)
    rest = values - high.astype(F32)
    middle = rest.astype(BF16)
    return high, middle, (rest - middle.astype(F32)).astype(BF16)


def result_kernel(dest_ref, back_ref, out_ref):
    peers, _, cap = back_ref.shape
    pieces = three_parts(back_ref[:, 0, :])
    step = 512
    for at in range(0, dest_ref.shape[1], step):
        dest = dest_ref[:, at : at + step]
        owner = dest // cap
        hot = one_hot(dest - owner * cap == iota((cap, step), 0))
        parts = [jnp.dot(part, hot, preferred_element_type=F32) for part in pieces]
        found = parts[0] + (parts[1] + parts[2])
        out_ref[:, at : at + step] = jnp.sum(jnp.where(owner == iota((peers, step), 0), found, 0.0), axis=0, keepdims=True)


def results(dest, back):
    return pl.pallas_call(
        result_kernel,
        out_shape=jax.ShapeDtypeStruct(dest.shape, F32),
        in_specs=whole(2),
        out_specs=whole(1)[0],
        compiler_params=pltpu.CompilerParams(vmem_limit_bytes=SMALL_VMEM),
        name="results",
    )(dest, back)


def cluster_best(pair):
    blocks, flags = pair
    peers, owned, most, width = blocks.shape
    slots = peers * most
    members = jnp.transpose(blocks, (1, 0, 2, 3)).reshape(owned, slots, width)
    valid = jnp.transpose(flags, (1, 0, 2)).reshape(owned, slots) > 0.5
    off_diagonal = jnp.logical_not(jnp.eye(slots, dtype=bool))

    def one_cluster(item):
        rows_of, valid_of = item
        gram = jnp.dot(rows_of, rows_of.T, preferred_element_type=jnp.float32)
        keep = valid_of[None, :] & off_diagonal
        return jnp.max(jnp.where(keep, gram, jnp.float32(-1.0)), axis=1)

    best = lax.map(one_cluster, (members, valid))
    return jnp.transpose(best.reshape(owned, peers, most), (1, 0, 2))


def roomy(labels, ranks, unit):
    count, width = unit.shape
    peers = lax.axis_size("rows")
    owned = CLUSTERS // peers
    cluster_hot = (labels[:, None] == jnp.arange(CLUSTERS, dtype=I32)[None, :]).astype(F32)
    rank_hot = (ranks[:, None] == jnp.arange(MOST, dtype=I32)[None, :]).astype(F32)
    numbered = rank_hot * jnp.arange(1, count + 1, dtype=F32)[:, None]
    filled = jnp.dot(cluster_hot.T, rank_hot, precision=EXACT)
    member_idx = jnp.dot(cluster_hot.T, numbered, precision=EXACT).astype(I32) - 1
    member_idx = jnp.where(member_idx < 0, count, member_idx).reshape(CLUSTERS * MOST)
    padded = jnp.concatenate([unit, jnp.zeros((1, width), BF16)], axis=0)
    outgoing = padded[member_idx].reshape(peers, owned, MOST, width)
    occupied = filled.astype(BF16).reshape(peers, owned, MOST)
    best = cluster_best((exchange(outgoing), exchange(occupied)))
    table = exchange(best).reshape(CLUSTERS, MOST)
    per_row = jnp.dot(cluster_hot, table, precision=EXACT)
    return jnp.sum(per_row * rank_hot, axis=1)


def exchange(blocks, groups=None):
    return lax.all_to_all(blocks, "rows", split_axis=0, concat_axis=0, tiled=True, axis_index_groups=groups)


def swap(block, number, peers):
    return lax.ppermute(block, "rows", [(i, i ^ number) for i in range(peers)])


def local(embeddings, cluster_id):
    count, width = embeddings.shape
    peers = lax.axis_size("rows")
    cap = -(-(count // peers + SLACK) // 16) * 16
    labels = cluster_id.reshape(1, count)
    counts = exchange(counted(labels, peers))
    ranks = ranked(labels)
    unit = unit_rows(embeddings)
    me = lax.axis_index("rows").reshape(1)
    dest, table = places(me, counts, labels, ranks, cap)

    half = peers // 2
    across = list(range(half, peers))
    leaving = packed(me, dest, unit, cap, peers, across[:EARLY])
    later, _ = lax.optimization_barrier((dest, leaving[0]))
    leaving += packed(me, later, unit, cap, peers, across[EARLY:])
    (inside,) = packed(me, later, unit, cap, peers, list(range(half)), half)
    arrived = [swap(block, number, peers) for block, number in zip(leaving, across)]
    inside, _, *arrived[:EARLY] = lax.optimization_barrier((inside, leaving[EARLY], *arrived[:EARLY]))
    inside = exchange(inside.reshape(half, cap, width), [list(range(half)), list(range(half, peers))])
    blocks = [inside.reshape(half * cap, width)] + arrived
    key_row, key_col, most = keys(me, table, cap)
    known = peers - LATE
    first = functools.partial(first_kernel, cap, known)
    best = call_bests(first, [], [key_row, key_col], blocks[: len(blocks) - LATE], known, known, cap)
    last = functools.partial(last_kernel, cap, known)
    best = call_bests(last, [me], [key_row, key_col, best], blocks, peers, LATE, cap)
    back = exchange(best)
    nearest = results(dest, back).reshape(count)
    return lax.cond(
        most[0, 0] > cap,
        lambda labels, ranks, unit, nearest: roomy(labels.reshape(count), ranks.reshape(count), unit),
        lambda labels, ranks, unit, nearest: nearest,
        labels, ranks, unit, nearest,
    )


def solution(mesh):
    return jax.shard_map(
        local,
        mesh=mesh,
        in_specs=(P(("groups", "rows"), None), P(("groups", "rows"), None)),
        out_specs=P(("groups", "rows")),
        check_vma=False,
    )
```

```python
import functools

import jax
import jax.numpy as jnp
import numpy as np
from jax import lax
from jax.experimental import pallas as pl
from jax.experimental.pallas import tpu as pltpu
from jax.sharding import PartitionSpec as P

CLUSTERS = 512
MOST = 16
LANES = 128
SLACK = 16
ROUNDS = 6
EARLY = 3
LATE = 3
EXACT = lax.Precision.HIGHEST
BF16, F32, I32 = jnp.bfloat16, jnp.float32, jnp.int32
VMEM_LIMIT = 24 * 1024 * 1024
SMALL_VMEM = 12 * 1024 * 1024
NT = (((1,), (1,)), ((), ()))


def iota(shape, dim):
    return lax.broadcasted_iota(I32, shape, dim)


def one_hot(mask):
    return jnp.where(mask, jnp.float32(1), jnp.float32(0)).astype(BF16)


def quotient(index, by, limit):
    numbers = np.arange(limit)
    for shift in range(8, 24):
        factor = -(-(1 << shift) // by)
        if limit * factor < 1 << 31 and np.array_equal(numbers * factor >> shift, numbers // by):
            return (index * factor) >> shift
    raise ValueError("no factor")


def whole(count):
    return [pl.BlockSpec(memory_space=pltpu.VMEM)] * count


def count_kernel(label_ref, count_ref):
    step = 512
    partial = jnp.zeros((CLUSTERS, LANES), F32)
    for at in range(0, label_ref.shape[1], step):
        hot = label_ref[:, at : at + step] == iota((CLUSTERS, step), 0)
        hot = jnp.where(hot, jnp.float32(1), jnp.float32(0))
        partial = functools.reduce(jnp.add, [hot[:, lane : lane + LANES] for lane in range(0, step, LANES)], partial)
    counts = jnp.sum(jnp.transpose(partial), axis=0, keepdims=True)
    count_ref[...] = jnp.broadcast_to(counts[None], count_ref.shape)


def counted(labels, peers):
    return pl.pallas_call(
        count_kernel,
        out_shape=jax.ShapeDtypeStruct((peers, 1, CLUSTERS), F32),
        in_specs=whole(1),
        out_specs=whole(1)[0],
        compiler_params=pltpu.CompilerParams(vmem_limit_bytes=SMALL_VMEM),
        name="counts",
    )(labels)


def rank_kernel(label_ref, rank_ref):
    step = 256
    tri = one_hot((iota((step, step + LANES), 0) < iota((step, step + LANES), 1)) | (iota((step, step + LANES), 1) >= step))
    running = jnp.zeros((CLUSTERS, LANES), F32)
    for at in range(0, label_ref.shape[1], step):
        hot = label_ref[:, at : at + step] == iota((CLUSTERS, step), 0)
        before = jnp.dot(one_hot(hot), tri, preferred_element_type=F32)
        here = before[:, :step] + jnp.concatenate([running] * (step // LANES), axis=1)
        rank_ref[:, at : at + step] = jnp.sum(jnp.where(hot, here, 0.0), axis=0, keepdims=True).astype(I32)
        running = running + before[:, step:]


def ranked(labels):
    return pl.pallas_call(
        rank_kernel,
        out_shape=jax.ShapeDtypeStruct(labels.shape, I32),
        in_specs=whole(1),
        out_specs=whole(1)[0],
        cost_estimate=pl.CostEstimate(flops=labels.shape[1] * CLUSTERS * 8, bytes_accessed=1 << 22, transcendentals=0),
        compiler_params=pltpu.CompilerParams(vmem_limit_bytes=SMALL_VMEM),
        name="ranks",
    )(labels)


def unit_kernel(rows_ref, unit_ref):
    values = rows_ref[...].astype(F32)
    total = jnp.sum(values * values, axis=1, keepdims=True)
    unit_ref[...] = (values * lax.rsqrt(total + 1e-06)).astype(BF16)


def unit_rows(embeddings):
    count, width = embeddings.shape
    step = min(512, count)
    spec = pl.BlockSpec((step, width), lambda i: (i, 0))
    return pl.pallas_call(
        unit_kernel,
        out_shape=jax.ShapeDtypeStruct((count, width), BF16),
        grid=(count // step,),
        in_specs=[spec],
        out_specs=spec,
        cost_estimate=pl.CostEstimate(flops=4 * count * width, bytes_accessed=4 * count * width, transcendentals=count),
        compiler_params=pltpu.CompilerParams(vmem_limit_bytes=SMALL_VMEM),
        name="unit",
    )(embeddings)


def swapped_evenly(table, peers):
    pieces = [table[:, at : at + LANES] for at in range(0, CLUSTERS, LANES)]
    lane = iota((1, LANES), 1)

    def over_laps(parts, combine):
        found = functools.reduce(combine, parts)
        shift = peers
        while shift < LANES:
            found = combine(found, pltpu.roll(found, shift, 1))
            shift *= 2
        return found

    bits = [1 << i for i in range(peers.bit_length() - 1)]
    for bit in (bits * ROUNDS)[:ROUNDS]:

        def partner(x):
            return jnp.where((lane & bit) == 0, pltpu.roll(x, LANES - bit, 1), pltpu.roll(x, bit, 1))

        load = over_laps([piece[:peers] for piece in pieces], jnp.add)
        excess = load - partner(load)
        others = [partner(piece) for piece in pieces]
        gains = []
        for piece, other in zip(pieces, others):
            moved = piece[:peers] - other[:peers]
            gains.append(jnp.sum(moved * (excess - moved), axis=0, keepdims=True))
        best = over_laps(gains, jnp.maximum)
        pieces = [
            jnp.where((gain == best) & (gain > 0.0), other, piece) for gain, other, piece in zip(gains, others, pieces)
        ]
    return jnp.concatenate(pieces, axis=1)


def offsets(table, peers):
    square = (CLUSTERS, CLUSTERS)
    bits = peers.bit_length() - 1
    first, second = iota(square, 0), iota(square, 1)
    earlier = one_hot((((first ^ second) & (peers - 1)) == 0) & ((first >> bits) < (second >> bits)))
    return jnp.dot(table[:peers].astype(BF16), earlier, preferred_element_type=F32)


def place_kernel(cap, me_ref, count_ref, label_ref, rank_ref, dest_ref, table_ref):
    me = me_ref[0]
    counts = count_ref[:, 0, :]
    peers = counts.shape[0]
    bits = peers.bit_length() - 1
    square = (CLUSTERS, CLUSTERS)
    total = jnp.sum(counts, axis=0, keepdims=True)
    total_col = jnp.transpose(jnp.broadcast_to(total, (LANES, CLUSTERS)))[:, :1]
    first, second = iota(square, 0), iota(square, 1)
    ahead = (total_col > total) | ((total_col == total) & (first < second))
    turn = (CLUSTERS - 1) - jnp.sum(jnp.where(ahead, 1.0, 0.0), axis=1, keepdims=True).astype(I32)
    place = jnp.where(((turn >> bits) & 1) == 0, turn, turn ^ (peers - 1))
    number = iota((8, CLUSTERS), 1)
    digits = jnp.where(iota((8, CLUSTERS), 0) == 0, number >> 4, number & 15).astype(F32)
    table = jnp.concatenate([counts, digits], axis=0).astype(BF16)
    table = jnp.dot(table, one_hot(place == second), preferred_element_type=F32)
    table = swapped_evenly(table, peers)
    table_ref[...] = table

    offset = offsets(table, peers)
    mine = jnp.sum(jnp.where(iota(counts.shape, 0) == me, offset, 0.0), axis=0, keepdims=True)
    base = mine + ((iota((1, CLUSTERS), 1) & (peers - 1)) * cap).astype(F32)
    cluster = table[peers : peers + 1] * 16.0 + table[peers + 1 : peers + 2]
    both = jnp.transpose(jnp.where(iota((LANES, CLUSTERS), 0) == 0, cluster, base))
    cluster_col, base_col = both[:, :1].astype(I32), both[:, 1:2]
    step = 512
    for at in range(0, label_ref.shape[1], step):
        hot = label_ref[:, at : at + step] == cluster_col
        slot = jnp.sum(jnp.where(hot, base_col, 0.0), axis=0, keepdims=True).astype(I32)
        dest_ref[:, at : at + step] = slot + rank_ref[:, at : at + step]


def places(me, counts, labels, ranks, cap):
    peers = counts.shape[0]
    return pl.pallas_call(
        functools.partial(place_kernel, cap),
        out_shape=(jax.ShapeDtypeStruct(labels.shape, I32), jax.ShapeDtypeStruct((peers + 8, CLUSTERS), F32)),
        in_specs=[pl.BlockSpec(memory_space=pltpu.SMEM)] + whole(3),
        out_specs=tuple(whole(2)),
        compiler_params=pltpu.CompilerParams(vmem_limit_bytes=SMALL_VMEM),
        name="places",
    )(me, counts, labels, ranks)


def owner_of(me, number, peers):
    half = peers // 2
    return (me & -half) + number if number < half else me ^ number


def sender_of(me, block, peers):
    half = peers // 2
    early = half - LATE
    inside = (me & -half) + block - early
    return jnp.where(block < early, me ^ (block + half), jnp.where(block < early + half, inside, me ^ block))


def pack_kernel(cap, peers, numbers, me_ref, dest_ref, unit_ref, *block_refs):
    me = me_ref[0]
    count = dest_ref.shape[1]
    per_ref = block_refs[0].shape[0] // cap
    group = 4
    for at in range(0, len(numbers), group):
        some = numbers[at : at + group]
        index = iota((len(some) * cap, 1), 0)
        slots = index
        for i, number in enumerate(some):
            shift = (owner_of(me, number, peers) - i) * cap
            slots = jnp.where((index >= i * cap) & (index < (i + 1) * cap), index + shift, slots)
        pick = one_hot(dest_ref[...] == slots)
        rows = jnp.dot(pick, unit_ref[...], preferred_element_type=F32).astype(BF16)
        for i in range(len(some)):
            block, within = divmod(at + i, per_ref)
            block_refs[block][within * cap : (within + 1) * cap, :] = rows[i * cap : (i + 1) * cap]


def packed(me, dest, unit, cap, peers, numbers, per_block=1):
    count, width = unit.shape
    rows = len(numbers) * cap
    blocks = len(numbers) // per_block
    return pl.pallas_call(
        functools.partial(pack_kernel, cap, peers, numbers),
        out_shape=tuple([jax.ShapeDtypeStruct((per_block * cap, width), BF16)] * blocks),
        in_specs=[pl.BlockSpec(memory_space=pltpu.SMEM)] + whole(2),
        out_specs=tuple(whole(blocks)),
        cost_estimate=pl.CostEstimate(
            flops=2 * rows * count * width, bytes_accessed=2 * width * (count + rows), transcendentals=0
        ),
        compiler_params=pltpu.CompilerParams(vmem_limit_bytes=VMEM_LIMIT),
        name="pack",
    )(me, dest, unit)


def key_kernel(cap, me_ref, table_ref, row_ref, col_ref, most_ref):
    me = me_ref[0]
    peers = table_ref.shape[0] - 8
    bits = peers.bit_length() - 1
    owned = CLUSTERS // peers
    slots = peers * cap
    ends = offsets(table_ref[...], peers) + table_ref[:peers]
    most_ref[...] = jnp.broadcast_to(jnp.max(ends, axis=(0, 1), keepdims=True), most_ref.shape)
    chosen = iota((LANES, CLUSTERS), 1) == (iota((LANES, CLUSTERS), 0) << bits) + me
    chosen = jnp.where(chosen, jnp.float32(1), jnp.float32(0))
    own = lax.dot_general(chosen, ends, NT, precision=EXACT, preferred_element_type=F32)
    own = jnp.where(iota(own.shape, 0) < owned, own, jnp.float32(1 << 20))

    index = iota((1, slots), 1)
    block = quotient(index, cap, slots)
    spot = (index - block * cap).astype(F32)
    from_peer = sender_of(me, block, peers) == iota((peers, slots), 0)
    from_peer = jnp.where(from_peer, jnp.float32(1), jnp.float32(0))
    ends = jnp.dot(own, from_peer, precision=EXACT, preferred_element_type=F32)
    row = jnp.sum(jnp.where(ends <= spot, 1.0, 0.0), axis=0, keepdims=True)
    row_ref[...] = row
    col_ref[...] = jnp.transpose(jnp.broadcast_to(row, (LANES, slots)))


def keys(me, table, cap):
    peers = table.shape[0] - 8
    slots = peers * cap
    return pl.pallas_call(
        functools.partial(key_kernel, cap),
        out_shape=(
            jax.ShapeDtypeStruct((1, slots), F32),
            jax.ShapeDtypeStruct((slots, LANES), F32),
            jax.ShapeDtypeStruct((8, LANES), F32),
        ),
        in_specs=[pl.BlockSpec(memory_space=pltpu.SMEM)] + whole(1),
        out_specs=tuple(whole(3)),
        cost_estimate=pl.CostEstimate(flops=1 << 36, bytes_accessed=1 << 22, transcendentals=0),
        compiler_params=pltpu.CompilerParams(vmem_limit_bytes=SMALL_VMEM),
        name="keys",
    )(me, table)


def rows_of(refs, cap, start, count):
    found, at = [], 0
    for ref in refs:
        blocks = ref.shape[0] // cap
        low, high = max(start, at), min(start + count, at + blocks)
        if low < high:
            found.append(ref[(low - at) * cap : (high - at) * cap, :])
        at += blocks
    return found[0] if len(found) == 1 else jnp.concatenate(found, axis=0)


def masked_parts(rows, columns, key_col, key_row, itself):
    gram = lax.dot_general(rows, columns, NT, preferred_element_type=F32)
    height, width = gram.shape
    parts = []
    for lane in range(0, width, LANES):
        wide = min(LANES, width - lane)
        part = gram[:, lane : lane + wide]
        keep = key_col[:, :wide] == key_row[:, lane : lane + wide]
        if -width < itself < height:
            keep = keep & (iota(part.shape, 0) - iota(part.shape, 1) != itself + lane)
        parts.append(jnp.where(keep, part, -1.0))
    return parts


def largest(parts):
    return jnp.concatenate([jnp.max(part, axis=0, keepdims=True) for part in parts], axis=1)


def first_kernel(cap, known, row_ref, col_ref, *refs):
    *block_refs, best_ref = refs
    tall, broad = max(1, 576 // cap), max(1, 432 // cap)
    for left in range(0, known, broad):
        count = min(broad, known - left)
        columns = rows_of(block_refs, cap, left, count)
        key_row = row_ref[:, left * cap : (left + count) * cap]
        best = jnp.full((1, count * cap), -1.0, F32)
        for upper in range(0, known, tall):
            rows = rows_of(block_refs, cap, upper, min(tall, known - upper))
            key_col = col_ref[upper * cap : upper * cap + rows.shape[0], :]
            best = jnp.maximum(best, largest(masked_parts(rows, columns, key_col, key_row, (left - upper) * cap)))
        for i in range(count):
            best_ref[left + i] = best[:, i * cap : (i + 1) * cap]


def next_kernel(cap, known, here, me_ref, row_ref, col_ref, before_ref, *refs):
    *block_refs, best_ref = refs
    me = me_ref[0]
    peers = row_ref.shape[1] // cap

    def place(block):
        return sender_of(me, block, peers) if here == peers else block

    tall = max(1, 576 // cap)
    columns = rows_of(block_refs, cap, known, here - known)
    key_row = row_ref[:, known * cap : here * cap]
    best = jnp.full((1, (here - known) * cap), -1.0, F32)
    for upper in range(0, here, tall):
        count = min(tall, here - upper)
        rows = rows_of(block_refs, cap, upper, count)
        key_col = col_ref[upper * cap : (upper + count) * cap, :]
        parts = masked_parts(rows, columns, key_col, key_row, (known - upper) * cap)
        best = jnp.maximum(best, largest(parts))
        if upper < known:
            tail = parts[-1]
            if tail.shape[1] < LANES:
                tail = jnp.concatenate([tail, jnp.full((count * cap, LANES - tail.shape[1]), -1.0, F32)], axis=1)
            side = functools.reduce(jnp.maximum, parts[:-1] + [tail])
            for i in range(min(count, known - upper)):
                across = jnp.max(jnp.transpose(side[i * cap : (i + 1) * cap]), axis=0, keepdims=True)
                best_ref[place(upper + i)] = jnp.maximum(before_ref[upper + i], across)
    for i in range(here - known):
        best_ref[place(known + i)] = best[:, i * cap : (i + 1) * cap]


def call_bests(kernel, scalars, arrays, blocks, out_blocks, fresh, cap):
    rows = sum(block.shape[0] for block in blocks)
    return pl.pallas_call(
        kernel,
        out_shape=jax.ShapeDtypeStruct((out_blocks, 1, cap), F32),
        in_specs=[pl.BlockSpec(memory_space=pltpu.SMEM)] * len(scalars) + whole(len(arrays) + len(blocks)),
        out_specs=whole(1)[0],
        cost_estimate=pl.CostEstimate(
            flops=2 * fresh * cap * rows * blocks[0].shape[1], bytes_accessed=1 << 23, transcendentals=0
        ),
        compiler_params=pltpu.CompilerParams(vmem_limit_bytes=VMEM_LIMIT),
        name="similar",
    )(*scalars, *arrays, *blocks)


def three_parts(values):
    high = values.astype(BF16)
    rest = values - high.astype(F32)
    middle = rest.astype(BF16)
    return high, middle, (rest - middle.astype(F32)).astype(BF16)


def result_kernel(dest_ref, back_ref, out_ref):
    peers, _, cap = back_ref.shape
    pieces = three_parts(back_ref[:, 0, :])
    step = 512
    for at in range(0, dest_ref.shape[1], step):
        dest = dest_ref[:, at : at + step]
        owner = dest // cap
        hot = one_hot(dest - owner * cap == iota((cap, step), 0))
        parts = [jnp.dot(part, hot, preferred_element_type=F32) for part in pieces]
        found = parts[0] + (parts[1] + parts[2])
        out_ref[:, at : at + step] = jnp.sum(jnp.where(owner == iota((peers, step), 0), found, 0.0), axis=0, keepdims=True)


def results(dest, back):
    return pl.pallas_call(
        result_kernel,
        out_shape=jax.ShapeDtypeStruct(dest.shape, F32),
        in_specs=whole(2),
        out_specs=whole(1)[0],
        compiler_params=pltpu.CompilerParams(vmem_limit_bytes=SMALL_VMEM),
        name="results",
    )(dest, back)


def cluster_best(pair):
    blocks, flags = pair
    peers, owned, most, width = blocks.shape
    slots = peers * most
    members = jnp.transpose(blocks, (1, 0, 2, 3)).reshape(owned, slots, width)
    valid = jnp.transpose(flags, (1, 0, 2)).reshape(owned, slots) > 0.5
    off_diagonal = jnp.logical_not(jnp.eye(slots, dtype=bool))

    def one_cluster(item):
        rows_of, valid_of = item
        gram = jnp.dot(rows_of, rows_of.T, preferred_element_type=jnp.float32)
        keep = valid_of[None, :] & off_diagonal
        return jnp.max(jnp.where(keep, gram, jnp.float32(-1.0)), axis=1)

    best = lax.map(one_cluster, (members, valid))
    return jnp.transpose(best.reshape(owned, peers, most), (1, 0, 2))


def roomy(labels, ranks, unit):
    count, width = unit.shape
    peers = lax.axis_size("rows")
    owned = CLUSTERS // peers
    cluster_hot = (labels[:, None] == jnp.arange(CLUSTERS, dtype=I32)[None, :]).astype(F32)
    rank_hot = (ranks[:, None] == jnp.arange(MOST, dtype=I32)[None, :]).astype(F32)
    numbered = rank_hot * jnp.arange(1, count + 1, dtype=F32)[:, None]
    filled = jnp.dot(cluster_hot.T, rank_hot, precision=EXACT)
    member_idx = jnp.dot(cluster_hot.T, numbered, precision=EXACT).astype(I32) - 1
    member_idx = jnp.where(member_idx < 0, count, member_idx).reshape(CLUSTERS * MOST)
    padded = jnp.concatenate([unit, jnp.zeros((1, width), BF16)], axis=0)
    outgoing = padded[member_idx].reshape(peers, owned, MOST, width)
    occupied = filled.astype(BF16).reshape(peers, owned, MOST)
    best = cluster_best((exchange(outgoing), exchange(occupied)))
    table = exchange(best).reshape(CLUSTERS, MOST)
    per_row = jnp.dot(cluster_hot, table, precision=EXACT)
    return jnp.sum(per_row * rank_hot, axis=1)


def exchange(blocks, groups=None):
    return lax.all_to_all(blocks, "rows", split_axis=0, concat_axis=0, tiled=True, axis_index_groups=groups)


def swap(block, number, peers):
    return lax.ppermute(block, "rows", [(i, i ^ number) for i in range(peers)])


def local(embeddings, cluster_id):
    count, width = embeddings.shape
    peers = lax.axis_size("rows")
    cap = -(-(count // peers + SLACK) // 16) * 16
    labels = cluster_id.reshape(1, count)
    counts = exchange(counted(labels, peers))
    ranks = ranked(labels)
    unit = unit_rows(embeddings)
    me = lax.axis_index("rows").reshape(1)
    dest, table = places(me, counts, labels, ranks, cap)

    half = peers // 2
    across = list(range(half, peers))
    leaving = packed(me, dest, unit, cap, peers, across[:EARLY])
    later, _ = lax.optimization_barrier((dest, leaving[0]))
    leaving += packed(me, later, unit, cap, peers, across[EARLY:])
    (inside,) = packed(me, later, unit, cap, peers, list(range(half)), half)
    arrived = [swap(block, number, peers) for block, number in zip(leaving, across)]
    inside, _, *arrived[:EARLY] = lax.optimization_barrier((inside, leaving[EARLY], *arrived[:EARLY]))
    inside = exchange(inside.reshape(half, cap, width), [list(range(half)), list(range(half, peers))])
    key_row, key_col, most = keys(me, table, cap)
    early = half - LATE
    blocks = arrived[:early] + [inside.reshape(half * cap, width)] + arrived[early:]
    first = functools.partial(first_kernel, cap, early)
    best = call_bests(first, [], [key_row, key_col], blocks[:early], early, early, cap)
    middle = functools.partial(next_kernel, cap, early, early + half)
    best = call_bests(middle, [me], [key_row, key_col, best], blocks[: early + 1], early + half, half, cap)
    last = functools.partial(next_kernel, cap, early + half, peers)
    best = call_bests(last, [me], [key_row, key_col, best], blocks, peers, LATE, cap)
    back = exchange(best)
    nearest = results(dest, back).reshape(count)
    return lax.cond(
        most[0, 0] > cap,
        lambda labels, ranks, unit, nearest: roomy(labels.reshape(count), ranks.reshape(count), unit),
        lambda labels, ranks, unit, nearest: nearest,
        labels, ranks, unit, nearest,
    )


def solution(mesh):
    return jax.shard_map(
        local,
        mesh=mesh,
        in_specs=(P(("groups", "rows"), None), P(("groups", "rows"), None)),
        out_specs=P(("groups", "rows")),
        check_vma=False,
    )
```

```python
import functools

import jax
import jax.numpy as jnp
import numpy as np
from jax import lax
from jax.experimental import pallas as pl
from jax.experimental.pallas import tpu as pltpu
from jax.sharding import PartitionSpec as P

CLUSTERS = 512
MOST = 16
LANES = 128
SLACK = 16
ROUNDS = 6
EARLY = 3
LATE = 3
EXACT = lax.Precision.HIGHEST
BF16, F32, I32 = jnp.bfloat16, jnp.float32, jnp.int32
VMEM_LIMIT = 24 * 1024 * 1024
SMALL_VMEM = 12 * 1024 * 1024
LARGE_VMEM = 60 * 1024 * 1024
NT = (((1,), (1,)), ((), ()))


def iota(shape, dim):
    return lax.broadcasted_iota(I32, shape, dim)


def one_hot(mask):
    return jnp.where(mask, jnp.float32(1), jnp.float32(0)).astype(BF16)


def quotient(index, by, limit):
    numbers = np.arange(limit)
    for shift in range(8, 24):
        factor = -(-(1 << shift) // by)
        if limit * factor < 1 << 31 and np.array_equal(numbers * factor >> shift, numbers // by):
            return (index * factor) >> shift
    raise ValueError("no factor")


def whole(count):
    return [pl.BlockSpec(memory_space=pltpu.VMEM)] * count


def count_kernel(label_ref, count_ref):
    step = 512
    partial = jnp.zeros((CLUSTERS, LANES), F32)
    for at in range(0, label_ref.shape[1], step):
        hot = label_ref[:, at : at + step] == iota((CLUSTERS, step), 0)
        hot = jnp.where(hot, jnp.float32(1), jnp.float32(0))
        partial = functools.reduce(jnp.add, [hot[:, lane : lane + LANES] for lane in range(0, step, LANES)], partial)
    counts = jnp.sum(jnp.transpose(partial), axis=0, keepdims=True)
    count_ref[...] = jnp.broadcast_to(counts[None], count_ref.shape)


def counted(labels, peers):
    return pl.pallas_call(
        count_kernel,
        out_shape=jax.ShapeDtypeStruct((peers, 1, CLUSTERS), F32),
        in_specs=whole(1),
        out_specs=whole(1)[0],
        compiler_params=pltpu.CompilerParams(vmem_limit_bytes=SMALL_VMEM),
        name="counts",
    )(labels)


def rank_kernel(label_ref, rank_ref):
    step = 256
    tri = one_hot((iota((step, step + LANES), 0) < iota((step, step + LANES), 1)) | (iota((step, step + LANES), 1) >= step))
    running = jnp.zeros((CLUSTERS, LANES), F32)
    for at in range(0, label_ref.shape[1], step):
        hot = label_ref[:, at : at + step] == iota((CLUSTERS, step), 0)
        before = jnp.dot(one_hot(hot), tri, preferred_element_type=F32)
        here = before[:, :step] + jnp.concatenate([running] * (step // LANES), axis=1)
        rank_ref[:, at : at + step] = jnp.sum(jnp.where(hot, here, 0.0), axis=0, keepdims=True).astype(I32)
        running = running + before[:, step:]


def ranked(labels):
    return pl.pallas_call(
        rank_kernel,
        out_shape=jax.ShapeDtypeStruct(labels.shape, I32),
        in_specs=whole(1),
        out_specs=whole(1)[0],
        cost_estimate=pl.CostEstimate(flops=labels.shape[1] * CLUSTERS * 8, bytes_accessed=1 << 22, transcendentals=0),
        compiler_params=pltpu.CompilerParams(vmem_limit_bytes=SMALL_VMEM),
        name="ranks",
    )(labels)


def unit_kernel(rows_ref, unit_ref):
    values = rows_ref[...].astype(F32)
    total = jnp.sum(values * values, axis=1, keepdims=True)
    unit_ref[...] = (values * lax.rsqrt(total + 1e-06)).astype(BF16)


def unit_rows(embeddings):
    count, width = embeddings.shape
    step = min(1024, count)
    spec = pl.BlockSpec((step, width), lambda i: (i, 0))
    return pl.pallas_call(
        unit_kernel,
        out_shape=jax.ShapeDtypeStruct((count, width), BF16),
        grid=(count // step,),
        in_specs=[spec],
        out_specs=spec,
        cost_estimate=pl.CostEstimate(flops=4 * count * width, bytes_accessed=4 * count * width, transcendentals=count),
        compiler_params=pltpu.CompilerParams(vmem_limit_bytes=LARGE_VMEM),
        name="unit",
    )(embeddings)


def swapped_evenly(table, peers):
    pieces = [table[:, at : at + LANES] for at in range(0, CLUSTERS, LANES)]
    lane = iota((1, LANES), 1)

    def over_laps(parts, combine):
        found = functools.reduce(combine, parts)
        shift = peers
        while shift < LANES:
            found = combine(found, pltpu.roll(found, shift, 1))
            shift *= 2
        return found

    bits = [1 << i for i in range(peers.bit_length() - 1)]
    for bit in (bits * ROUNDS)[:ROUNDS]:

        def partner(x):
            return jnp.where((lane & bit) == 0, pltpu.roll(x, LANES - bit, 1), pltpu.roll(x, bit, 1))

        load = over_laps([piece[:peers] for piece in pieces], jnp.add)
        excess = load - partner(load)
        others = [partner(piece) for piece in pieces]
        gains = []
        for piece, other in zip(pieces, others):
            moved = piece[:peers] - other[:peers]
            gains.append(jnp.sum(moved * (excess - moved), axis=0, keepdims=True))
        best = over_laps(gains, jnp.maximum)
        pieces = [
            jnp.where((gain == best) & (gain > 0.0), other, piece) for gain, other, piece in zip(gains, others, pieces)
        ]
    return jnp.concatenate(pieces, axis=1)


def offsets(table, peers):
    square = (CLUSTERS, CLUSTERS)
    bits = peers.bit_length() - 1
    first, second = iota(square, 0), iota(square, 1)
    earlier = one_hot((((first ^ second) & (peers - 1)) == 0) & ((first >> bits) < (second >> bits)))
    return jnp.dot(table[:peers].astype(BF16), earlier, preferred_element_type=F32)


def place_kernel(cap, me_ref, count_ref, label_ref, rank_ref, dest_ref, table_ref):
    me = me_ref[0]
    counts = count_ref[:, 0, :]
    peers = counts.shape[0]
    bits = peers.bit_length() - 1
    square = (CLUSTERS, CLUSTERS)
    total = jnp.sum(counts, axis=0, keepdims=True)
    total_col = jnp.transpose(jnp.broadcast_to(total, (LANES, CLUSTERS)))[:, :1]
    first, second = iota(square, 0), iota(square, 1)
    ahead = (total_col > total) | ((total_col == total) & (first < second))
    turn = (CLUSTERS - 1) - jnp.sum(jnp.where(ahead, 1.0, 0.0), axis=1, keepdims=True).astype(I32)
    place = jnp.where(((turn >> bits) & 1) == 0, turn, turn ^ (peers - 1))
    number = iota((8, CLUSTERS), 1)
    digits = jnp.where(iota((8, CLUSTERS), 0) == 0, number >> 4, number & 15).astype(F32)
    table = jnp.concatenate([counts, digits], axis=0).astype(BF16)
    table = jnp.dot(table, one_hot(place == second), preferred_element_type=F32)
    table = swapped_evenly(table, peers)
    table_ref[...] = table

    offset = offsets(table, peers)
    mine = jnp.sum(jnp.where(iota(counts.shape, 0) == me, offset, 0.0), axis=0, keepdims=True)
    base = mine + ((iota((1, CLUSTERS), 1) & (peers - 1)) * cap).astype(F32)
    cluster = table[peers : peers + 1] * 16.0 + table[peers + 1 : peers + 2]
    both = jnp.transpose(jnp.where(iota((LANES, CLUSTERS), 0) == 0, cluster, base))
    cluster_col, base_col = both[:, :1].astype(I32), both[:, 1:2]
    step = 512
    for at in range(0, label_ref.shape[1], step):
        hot = label_ref[:, at : at + step] == cluster_col
        slot = jnp.sum(jnp.where(hot, base_col, 0.0), axis=0, keepdims=True).astype(I32)
        dest_ref[:, at : at + step] = slot + rank_ref[:, at : at + step]


def owner_of(me, number, peers):
    half = peers // 2
    return (me & -half) + number if number < half else me ^ number


def sender_of(me, block, peers):
    half = peers // 2
    early = half - LATE
    inside = (me & -half) + block - early
    return jnp.where(block < early, me ^ (block + half), jnp.where(block < early + half, inside, me ^ block))


def pick_blocks(cap, peers, numbers, me, dest, unit_ref, block_refs):
    per_ref = block_refs[0].shape[0] // cap
    group = 4
    for at in range(0, len(numbers), group):
        some = numbers[at : at + group]
        index = iota((len(some) * cap, 1), 0)
        slots = index
        for i, number in enumerate(some):
            shift = (owner_of(me, number, peers) - i) * cap
            slots = jnp.where((index >= i * cap) & (index < (i + 1) * cap), index + shift, slots)
        pick = one_hot(dest == slots)
        rows = jnp.dot(pick, unit_ref[...], preferred_element_type=F32).astype(BF16)
        for i in range(len(some)):
            block, within = divmod(at + i, per_ref)
            block_refs[block][within * cap : (within + 1) * cap, :] = rows[i * cap : (i + 1) * cap]


def pack_kernel(cap, peers, numbers, me_ref, dest_ref, unit_ref, *block_refs):
    pick_blocks(cap, peers, numbers, me_ref[0], dest_ref[...], unit_ref, block_refs)


def place_pack_kernel(cap, peers, numbers, me_ref, count_ref, label_ref, rank_ref, unit_ref, dest_ref, table_ref, *refs):
    *block_refs, held, arrived = refs
    copy = pltpu.make_async_copy(unit_ref, held, arrived)
    copy.start()
    place_kernel(cap, me_ref, count_ref, label_ref, rank_ref, dest_ref, table_ref)
    copy.wait()
    pick_blocks(cap, peers, numbers, me_ref[0], dest_ref[...], held, block_refs)


def places_and_packed(me, counts, labels, ranks, unit, cap, numbers):
    peers = counts.shape[0]
    width = unit.shape[1]
    dest, table, *blocks = pl.pallas_call(
        functools.partial(place_pack_kernel, cap, peers, numbers),
        out_shape=(
            jax.ShapeDtypeStruct(labels.shape, I32),
            jax.ShapeDtypeStruct((peers + 8, CLUSTERS), F32),
            *[jax.ShapeDtypeStruct((cap, width), BF16)] * len(numbers),
        ),
        in_specs=[pl.BlockSpec(memory_space=pltpu.SMEM)] + whole(3) + [pl.BlockSpec(memory_space=pl.ANY)],
        out_specs=tuple(whole(2 + len(numbers))),
        scratch_shapes=[pltpu.VMEM(unit.shape, BF16), pltpu.SemaphoreType.DMA(())],
        compiler_params=pltpu.CompilerParams(vmem_limit_bytes=VMEM_LIMIT),
        name="places",
    )(me, counts, labels, ranks, unit)
    return dest, table, blocks


def packed(me, dest, unit, cap, peers, numbers, per_block=1):
    count, width = unit.shape
    rows = len(numbers) * cap
    blocks = len(numbers) // per_block
    return pl.pallas_call(
        functools.partial(pack_kernel, cap, peers, numbers),
        out_shape=tuple([jax.ShapeDtypeStruct((per_block * cap, width), BF16)] * blocks),
        in_specs=[pl.BlockSpec(memory_space=pltpu.SMEM)] + whole(2),
        out_specs=tuple(whole(blocks)),
        cost_estimate=pl.CostEstimate(
            flops=2 * rows * count * width, bytes_accessed=2 * width * (count + rows), transcendentals=0
        ),
        compiler_params=pltpu.CompilerParams(vmem_limit_bytes=VMEM_LIMIT),
        name="pack",
    )(me, dest, unit)


def key_kernel(cap, me_ref, table_ref, row_ref, col_ref, most_ref):
    me = me_ref[0]
    peers = table_ref.shape[0] - 8
    bits = peers.bit_length() - 1
    owned = CLUSTERS // peers
    slots = peers * cap
    ends = offsets(table_ref[...], peers) + table_ref[:peers]
    most_ref[...] = jnp.broadcast_to(jnp.max(ends, axis=(0, 1), keepdims=True), most_ref.shape)
    chosen = iota((LANES, CLUSTERS), 1) == (iota((LANES, CLUSTERS), 0) << bits) + me
    chosen = jnp.where(chosen, jnp.float32(1), jnp.float32(0))
    own = lax.dot_general(chosen, ends, NT, precision=EXACT, preferred_element_type=F32)
    own = jnp.where(iota(own.shape, 0) < owned, own, jnp.float32(1 << 20))

    index = iota((1, slots), 1)
    block = quotient(index, cap, slots)
    spot = (index - block * cap).astype(F32)
    from_peer = sender_of(me, block, peers) == iota((peers, slots), 0)
    from_peer = jnp.where(from_peer, jnp.float32(1), jnp.float32(0))
    ends = jnp.dot(own, from_peer, precision=EXACT, preferred_element_type=F32)
    row = jnp.sum(jnp.where(ends <= spot, 1.0, 0.0), axis=0, keepdims=True)
    row_ref[...] = row
    col_ref[...] = jnp.transpose(jnp.broadcast_to(row, (LANES, slots)))


def keys(me, table, cap):
    peers = table.shape[0] - 8
    slots = peers * cap
    return pl.pallas_call(
        functools.partial(key_kernel, cap),
        out_shape=(
            jax.ShapeDtypeStruct((1, slots), F32),
            jax.ShapeDtypeStruct((slots, LANES), F32),
            jax.ShapeDtypeStruct((8, LANES), F32),
        ),
        in_specs=[pl.BlockSpec(memory_space=pltpu.SMEM)] + whole(1),
        out_specs=tuple(whole(3)),
        cost_estimate=pl.CostEstimate(flops=1 << 36, bytes_accessed=1 << 22, transcendentals=0),
        compiler_params=pltpu.CompilerParams(vmem_limit_bytes=SMALL_VMEM),
        name="keys",
    )(me, table)


def rows_of(refs, cap, start, count):
    found, at = [], 0
    for ref in refs:
        blocks = ref.shape[0] // cap
        low, high = max(start, at), min(start + count, at + blocks)
        if low < high:
            found.append(ref[(low - at) * cap : (high - at) * cap, :])
        at += blocks
    return found[0] if len(found) == 1 else jnp.concatenate(found, axis=0)


def masked_parts(rows, columns, key_col, key_row, itself):
    gram = lax.dot_general(rows, columns, NT, preferred_element_type=F32)
    height, width = gram.shape
    parts = []
    for lane in range(0, width, LANES):
        wide = min(LANES, width - lane)
        part = gram[:, lane : lane + wide]
        keep = key_col[:, :wide] == key_row[:, lane : lane + wide]
        if -width < itself < height:
            keep = keep & (iota(part.shape, 0) - iota(part.shape, 1) != itself + lane)
        parts.append(jnp.where(keep, part, -1.0))
    return parts


def largest(parts):
    return jnp.concatenate([jnp.max(part, axis=0, keepdims=True) for part in parts], axis=1)


def first_kernel(cap, known, row_ref, col_ref, *refs):
    *block_refs, best_ref = refs
    tall, broad = max(1, 576 // cap), max(1, 432 // cap)
    for left in range(0, known, broad):
        count = min(broad, known - left)
        columns = rows_of(block_refs, cap, left, count)
        key_row = row_ref[:, left * cap : (left + count) * cap]
        best = jnp.full((1, count * cap), -1.0, F32)
        for upper in range(0, known, tall):
            rows = rows_of(block_refs, cap, upper, min(tall, known - upper))
            key_col = col_ref[upper * cap : upper * cap + rows.shape[0], :]
            best = jnp.maximum(best, largest(masked_parts(rows, columns, key_col, key_row, (left - upper) * cap)))
        for i in range(count):
            best_ref[left + i] = best[:, i * cap : (i + 1) * cap]


def next_kernel(cap, known, here, me_ref, row_ref, col_ref, before_ref, *refs):
    *block_refs, best_ref = refs
    me = me_ref[0]
    peers = row_ref.shape[1] // cap

    def place(block):
        return sender_of(me, block, peers) if here == peers else block

    tall = max(1, 576 // cap)
    columns = rows_of(block_refs, cap, known, here - known)
    key_row = row_ref[:, known * cap : here * cap]
    best = jnp.full((1, (here - known) * cap), -1.0, F32)
    for upper in range(0, here, tall):
        count = min(tall, here - upper)
        rows = rows_of(block_refs, cap, upper, count)
        key_col = col_ref[upper * cap : (upper + count) * cap, :]
        parts = masked_parts(rows, columns, key_col, key_row, (known - upper) * cap)
        best = jnp.maximum(best, largest(parts))
        if upper < known:
            tail = parts[-1]
            if tail.shape[1] < LANES:
                tail = jnp.concatenate([tail, jnp.full((count * cap, LANES - tail.shape[1]), -1.0, F32)], axis=1)
            side = functools.reduce(jnp.maximum, parts[:-1] + [tail])
            for i in range(min(count, known - upper)):
                across = jnp.max(jnp.transpose(side[i * cap : (i + 1) * cap]), axis=0, keepdims=True)
                best_ref[place(upper + i)] = jnp.maximum(before_ref[upper + i], across)
    for i in range(here - known):
        best_ref[place(known + i)] = best[:, i * cap : (i + 1) * cap]


def call_bests(kernel, scalars, arrays, blocks, out_blocks, fresh, cap):
    rows = sum(block.shape[0] for block in blocks)
    return pl.pallas_call(
        kernel,
        out_shape=jax.ShapeDtypeStruct((out_blocks, 1, cap), F32),
        in_specs=[pl.BlockSpec(memory_space=pltpu.SMEM)] * len(scalars) + whole(len(arrays) + len(blocks)),
        out_specs=whole(1)[0],
        cost_estimate=pl.CostEstimate(
            flops=2 * fresh * cap * rows * blocks[0].shape[1], bytes_accessed=1 << 23, transcendentals=0
        ),
        compiler_params=pltpu.CompilerParams(vmem_limit_bytes=VMEM_LIMIT),
        name="similar",
    )(*scalars, *arrays, *blocks)


def three_parts(values):
    high = values.astype(BF16)
    rest = values - high.astype(F32)
    middle = rest.astype(BF16)
    return high, middle, (rest - middle.astype(F32)).astype(BF16)


def result_kernel(dest_ref, back_ref, out_ref):
    peers, _, cap = back_ref.shape
    pieces = three_parts(back_ref[:, 0, :])
    step = 512
    for at in range(0, dest_ref.shape[1], step):
        dest = dest_ref[:, at : at + step]
        owner = dest // cap
        hot = one_hot(dest - owner * cap == iota((cap, step), 0))
        parts = [jnp.dot(part, hot, preferred_element_type=F32) for part in pieces]
        found = parts[0] + (parts[1] + parts[2])
        out_ref[:, at : at + step] = jnp.sum(jnp.where(owner == iota((peers, step), 0), found, 0.0), axis=0, keepdims=True)


def results(dest, back):
    return pl.pallas_call(
        result_kernel,
        out_shape=jax.ShapeDtypeStruct(dest.shape, F32),
        in_specs=whole(2),
        out_specs=whole(1)[0],
        compiler_params=pltpu.CompilerParams(vmem_limit_bytes=SMALL_VMEM),
        name="results",
    )(dest, back)


def cluster_best(pair):
    blocks, flags = pair
    peers, owned, most, width = blocks.shape
    slots = peers * most
    members = jnp.transpose(blocks, (1, 0, 2, 3)).reshape(owned, slots, width)
    valid = jnp.transpose(flags, (1, 0, 2)).reshape(owned, slots) > 0.5
    off_diagonal = jnp.logical_not(jnp.eye(slots, dtype=bool))

    def one_cluster(item):
        rows_of, valid_of = item
        gram = jnp.dot(rows_of, rows_of.T, preferred_element_type=jnp.float32)
        keep = valid_of[None, :] & off_diagonal
        return jnp.max(jnp.where(keep, gram, jnp.float32(-1.0)), axis=1)

    best = lax.map(one_cluster, (members, valid))
    return jnp.transpose(best.reshape(owned, peers, most), (1, 0, 2))


def roomy(labels, ranks, unit):
    count, width = unit.shape
    peers = lax.axis_size("rows")
    owned = CLUSTERS // peers
    cluster_hot = (labels[:, None] == jnp.arange(CLUSTERS, dtype=I32)[None, :]).astype(F32)
    rank_hot = (ranks[:, None] == jnp.arange(MOST, dtype=I32)[None, :]).astype(F32)
    numbered = rank_hot * jnp.arange(1, count + 1, dtype=F32)[:, None]
    filled = jnp.dot(cluster_hot.T, rank_hot, precision=EXACT)
    member_idx = jnp.dot(cluster_hot.T, numbered, precision=EXACT).astype(I32) - 1
    member_idx = jnp.where(member_idx < 0, count, member_idx).reshape(CLUSTERS * MOST)
    padded = jnp.concatenate([unit, jnp.zeros((1, width), BF16)], axis=0)
    outgoing = padded[member_idx].reshape(peers, owned, MOST, width)
    occupied = filled.astype(BF16).reshape(peers, owned, MOST)
    best = cluster_best((exchange(outgoing), exchange(occupied)))
    table = exchange(best).reshape(CLUSTERS, MOST)
    per_row = jnp.dot(cluster_hot, table, precision=EXACT)
    return jnp.sum(per_row * rank_hot, axis=1)


def exchange(blocks, groups=None):
    return lax.all_to_all(blocks, "rows", split_axis=0, concat_axis=0, tiled=True, axis_index_groups=groups)


def swap(block, number, peers):
    return lax.ppermute(block, "rows", [(i, i ^ number) for i in range(peers)])


def local(embeddings, cluster_id):
    count, width = embeddings.shape
    peers = lax.axis_size("rows")
    cap = -(-(count // peers + SLACK) // 16) * 16
    labels = cluster_id.reshape(1, count)
    counts = exchange(counted(labels, peers))
    ranks = ranked(labels)
    unit = unit_rows(embeddings)
    me = lax.axis_index("rows").reshape(1)

    half = peers // 2
    across = list(range(half, peers))
    dest, table, leaving = places_and_packed(me, counts, labels, ranks, unit, cap, across[:EARLY])
    later, _ = lax.optimization_barrier((dest, leaving[0]))
    leaving += list(packed(me, later, unit, cap, peers, across[EARLY:]))
    (inside,) = packed(me, later, unit, cap, peers, list(range(half)), half)
    arrived = [swap(block, number, peers) for block, number in zip(leaving, across)]
    inside, _, *arrived[:EARLY] = lax.optimization_barrier((inside, leaving[EARLY], *arrived[:EARLY]))
    inside = exchange(inside.reshape(half, cap, width), [list(range(half)), list(range(half, peers))])
    key_row, key_col, most = keys(me, table, cap)
    early = half - LATE
    blocks = arrived[:early] + [inside.reshape(half * cap, width)] + arrived[early:]
    first = functools.partial(first_kernel, cap, early)
    best = call_bests(first, [], [key_row, key_col], blocks[:early], early, early, cap)
    middle = functools.partial(next_kernel, cap, early, early + half)
    best = call_bests(middle, [me], [key_row, key_col, best], blocks[: early + 1], early + half, half, cap)
    last = functools.partial(next_kernel, cap, early + half, peers)
    best = call_bests(last, [me], [key_row, key_col, best], blocks, peers, LATE, cap)
    back = exchange(best)
    nearest = results(dest, back).reshape(count)
    return lax.cond(
        most[0, 0] > cap,
        lambda labels, ranks, unit, nearest: roomy(labels.reshape(count), ranks.reshape(count), unit),
        lambda labels, ranks, unit, nearest: nearest,
        labels, ranks, unit, nearest,
    )


def solution(mesh):
    return jax.shard_map(
        local,
        mesh=mesh,
        in_specs=(P(("groups", "rows"), None), P(("groups", "rows"), None)),
        out_specs=P(("groups", "rows")),
        check_vma=False,
    )
```

```python
import functools

import jax
import jax.numpy as jnp
import numpy as np
from jax import lax
from jax.experimental import pallas as pl
from jax.experimental.pallas import tpu as pltpu
from jax.sharding import PartitionSpec as P

CLUSTERS = 512
MOST = 16
LANES = 128
SLACK = 16
ROUNDS = 6
EARLY = 3
LATE = 3
EXACT = lax.Precision.HIGHEST
BF16, F32, I32 = jnp.bfloat16, jnp.float32, jnp.int32
VMEM_LIMIT = 24 * 1024 * 1024
SMALL_VMEM = 12 * 1024 * 1024
LARGE_VMEM = 60 * 1024 * 1024
NT = (((1,), (1,)), ((), ()))


def iota(shape, dim):
    return lax.broadcasted_iota(I32, shape, dim)


def one_hot(mask):
    return jnp.where(mask, jnp.float32(1), jnp.float32(0)).astype(BF16)


def quotient(index, by, limit):
    numbers = np.arange(limit)
    for shift in range(8, 24):
        factor = -(-(1 << shift) // by)
        if limit * factor < 1 << 31 and np.array_equal(numbers * factor >> shift, numbers // by):
            return (index * factor) >> shift
    raise ValueError("no factor")


def whole(count):
    return [pl.BlockSpec(memory_space=pltpu.VMEM)] * count


def count_kernel(label_ref, count_ref):
    step = 512
    partial = jnp.zeros((CLUSTERS, LANES), F32)
    for at in range(0, label_ref.shape[1], step):
        hot = label_ref[:, at : at + step] == iota((CLUSTERS, step), 0)
        hot = jnp.where(hot, jnp.float32(1), jnp.float32(0))
        partial = functools.reduce(jnp.add, [hot[:, lane : lane + LANES] for lane in range(0, step, LANES)], partial)
    counts = jnp.sum(jnp.transpose(partial), axis=0, keepdims=True)
    count_ref[...] = jnp.broadcast_to(counts[None], count_ref.shape)


def counted(labels, peers):
    return pl.pallas_call(
        count_kernel,
        out_shape=jax.ShapeDtypeStruct((peers, 1, CLUSTERS), F32),
        in_specs=whole(1),
        out_specs=whole(1)[0],
        compiler_params=pltpu.CompilerParams(vmem_limit_bytes=SMALL_VMEM),
        name="counts",
    )(labels)


def rank_kernel(label_ref, rank_ref):
    step = 256
    tri = one_hot((iota((step, step + LANES), 0) < iota((step, step + LANES), 1)) | (iota((step, step + LANES), 1) >= step))
    running = jnp.zeros((CLUSTERS, LANES), F32)
    for at in range(0, label_ref.shape[1], step):
        hot = label_ref[:, at : at + step] == iota((CLUSTERS, step), 0)
        before = jnp.dot(one_hot(hot), tri, preferred_element_type=F32)
        here = before[:, :step] + jnp.concatenate([running] * (step // LANES), axis=1)
        rank_ref[:, at : at + step] = jnp.sum(jnp.where(hot, here, 0.0), axis=0, keepdims=True).astype(I32)
        running = running + before[:, step:]


def ranked(labels):
    return pl.pallas_call(
        rank_kernel,
        out_shape=jax.ShapeDtypeStruct(labels.shape, I32),
        in_specs=whole(1),
        out_specs=whole(1)[0],
        cost_estimate=pl.CostEstimate(flops=labels.shape[1] * CLUSTERS * 8, bytes_accessed=1 << 22, transcendentals=0),
        compiler_params=pltpu.CompilerParams(vmem_limit_bytes=SMALL_VMEM),
        name="ranks",
    )(labels)


def unit_kernel(rows_ref, unit_ref):
    values = rows_ref[...].astype(F32)
    total = jnp.sum(values * values, axis=1, keepdims=True)
    unit_ref[...] = (values * lax.rsqrt(total + 1e-06)).astype(BF16)


def unit_rows(embeddings):
    count, width = embeddings.shape
    step = min(1024, count)
    spec = pl.BlockSpec((step, width), lambda i: (i, 0))
    return pl.pallas_call(
        unit_kernel,
        out_shape=jax.ShapeDtypeStruct((count, width), BF16),
        grid=(count // step,),
        in_specs=[spec],
        out_specs=spec,
        cost_estimate=pl.CostEstimate(flops=4 * count * width, bytes_accessed=4 * count * width, transcendentals=count),
        compiler_params=pltpu.CompilerParams(vmem_limit_bytes=LARGE_VMEM),
        name="unit",
    )(embeddings)


def swapped_evenly(table, peers):
    pieces = [table[:, at : at + LANES] for at in range(0, CLUSTERS, LANES)]
    lane = iota((1, LANES), 1)

    def over_laps(parts, combine):
        found = functools.reduce(combine, parts)
        shift = peers
        while shift < LANES:
            found = combine(found, pltpu.roll(found, shift, 1))
            shift *= 2
        return found

    bits = [1 << i for i in range(peers.bit_length() - 1)]
    for bit in (bits * ROUNDS)[:ROUNDS]:

        def partner(x):
            return jnp.where((lane & bit) == 0, pltpu.roll(x, LANES - bit, 1), pltpu.roll(x, bit, 1))

        load = over_laps([piece[:peers] for piece in pieces], jnp.add)
        excess = load - partner(load)
        others = [partner(piece) for piece in pieces]
        gains = []
        for piece, other in zip(pieces, others):
            moved = piece[:peers] - other[:peers]
            gains.append(jnp.sum(moved * (excess - moved), axis=0, keepdims=True))
        best = over_laps(gains, jnp.maximum)
        pieces = [
            jnp.where((gain == best) & (gain > 0.0), other, piece) for gain, other, piece in zip(gains, others, pieces)
        ]
    return jnp.concatenate(pieces, axis=1)


def offsets(table, peers):
    square = (CLUSTERS, CLUSTERS)
    bits = peers.bit_length() - 1
    first, second = iota(square, 0), iota(square, 1)
    earlier = one_hot((((first ^ second) & (peers - 1)) == 0) & ((first >> bits) < (second >> bits)))
    return jnp.dot(table[:peers].astype(BF16), earlier, preferred_element_type=F32)


def place_kernel(cap, me_ref, count_ref, label_ref, rank_ref, dest_ref, table_ref):
    me = me_ref[0]
    counts = count_ref[:, 0, :]
    peers = counts.shape[0]
    bits = peers.bit_length() - 1
    square = (CLUSTERS, CLUSTERS)
    total = jnp.sum(counts, axis=0, keepdims=True)
    total_col = jnp.transpose(jnp.broadcast_to(total, (LANES, CLUSTERS)))[:, :1]
    first, second = iota(square, 0), iota(square, 1)
    ahead = (total_col > total) | ((total_col == total) & (first < second))
    turn = (CLUSTERS - 1) - jnp.sum(jnp.where(ahead, 1.0, 0.0), axis=1, keepdims=True).astype(I32)
    place = jnp.where(((turn >> bits) & 1) == 0, turn, turn ^ (peers - 1))
    number = iota((8, CLUSTERS), 1)
    digits = jnp.where(iota((8, CLUSTERS), 0) == 0, number >> 4, number & 15).astype(F32)
    table = jnp.concatenate([counts, digits], axis=0).astype(BF16)
    table = jnp.dot(table, one_hot(place == second), preferred_element_type=F32)
    table = swapped_evenly(table, peers)
    table_ref[...] = table

    offset = offsets(table, peers)
    mine = jnp.sum(jnp.where(iota(counts.shape, 0) == me, offset, 0.0), axis=0, keepdims=True)
    base = mine + ((iota((1, CLUSTERS), 1) & (peers - 1)) * cap).astype(F32)
    cluster = table[peers : peers + 1] * 16.0 + table[peers + 1 : peers + 2]
    both = jnp.transpose(jnp.where(iota((LANES, CLUSTERS), 0) == 0, cluster, base))
    cluster_col, base_col = both[:, :1].astype(I32), both[:, 1:2]
    step = 512
    for at in range(0, label_ref.shape[1], step):
        hot = label_ref[:, at : at + step] == cluster_col
        slot = jnp.sum(jnp.where(hot, base_col, 0.0), axis=0, keepdims=True).astype(I32)
        dest_ref[:, at : at + step] = slot + rank_ref[:, at : at + step]


def owner_of(me, number, peers):
    half = peers // 2
    return (me & -half) + number if number < half else me ^ number


def sender_of(me, block, peers):
    half = peers // 2
    early = half - LATE
    inside = (me & -half) + block - early
    return jnp.where(block < early, me ^ (block + half), jnp.where(block < early + half, inside, me ^ block))


def pick_blocks(cap, peers, numbers, me, dest, unit_ref, block_refs):
    per_ref = block_refs[0].shape[0] // cap
    group = 4
    for at in range(0, len(numbers), group):
        some = numbers[at : at + group]
        index = iota((len(some) * cap, 1), 0)
        slots = index
        for i, number in enumerate(some):
            shift = (owner_of(me, number, peers) - i) * cap
            slots = jnp.where((index >= i * cap) & (index < (i + 1) * cap), index + shift, slots)
        pick = one_hot(dest == slots)
        rows = jnp.dot(pick, unit_ref[...], preferred_element_type=F32).astype(BF16)
        for i in range(len(some)):
            block, within = divmod(at + i, per_ref)
            block_refs[block][within * cap : (within + 1) * cap, :] = rows[i * cap : (i + 1) * cap]


def pack_kernel(cap, peers, numbers, me_ref, dest_ref, unit_ref, *block_refs):
    pick_blocks(cap, peers, numbers, me_ref[0], dest_ref[...], unit_ref, block_refs)


def place_pack_kernel(cap, peers, numbers, me_ref, count_ref, label_ref, rank_ref, unit_ref, dest_ref, table_ref, *refs):
    *block_refs, held, arrived = refs
    copy = pltpu.make_async_copy(unit_ref, held, arrived)
    copy.start()
    place_kernel(cap, me_ref, count_ref, label_ref, rank_ref, dest_ref, table_ref)
    copy.wait()
    pick_blocks(cap, peers, numbers, me_ref[0], dest_ref[...], held, block_refs)


def places_and_packed(me, counts, labels, ranks, unit, cap, numbers):
    peers = counts.shape[0]
    width = unit.shape[1]
    dest, table, *blocks = pl.pallas_call(
        functools.partial(place_pack_kernel, cap, peers, numbers),
        out_shape=(
            jax.ShapeDtypeStruct(labels.shape, I32),
            jax.ShapeDtypeStruct((peers + 8, CLUSTERS), F32),
            *[jax.ShapeDtypeStruct((cap, width), BF16)] * len(numbers),
        ),
        in_specs=[pl.BlockSpec(memory_space=pltpu.SMEM)] + whole(3) + [pl.BlockSpec(memory_space=pl.ANY)],
        out_specs=tuple(whole(2 + len(numbers))),
        scratch_shapes=[pltpu.VMEM(unit.shape, BF16), pltpu.SemaphoreType.DMA(())],
        compiler_params=pltpu.CompilerParams(vmem_limit_bytes=VMEM_LIMIT),
        name="places",
    )(me, counts, labels, ranks, unit)
    return dest, table, blocks


def packed(me, dest, unit, cap, peers, numbers, per_block=1):
    count, width = unit.shape
    rows = len(numbers) * cap
    blocks = len(numbers) // per_block
    return pl.pallas_call(
        functools.partial(pack_kernel, cap, peers, numbers),
        out_shape=tuple([jax.ShapeDtypeStruct((per_block * cap, width), BF16)] * blocks),
        in_specs=[pl.BlockSpec(memory_space=pltpu.SMEM)] + whole(2),
        out_specs=tuple(whole(blocks)),
        cost_estimate=pl.CostEstimate(
            flops=2 * rows * count * width, bytes_accessed=2 * width * (count + rows), transcendentals=0
        ),
        compiler_params=pltpu.CompilerParams(vmem_limit_bytes=VMEM_LIMIT),
        name="pack",
    )(me, dest, unit)


def key_kernel(cap, me_ref, table_ref, row_ref, col_ref, most_ref):
    me = me_ref[0]
    peers = table_ref.shape[0] - 8
    bits = peers.bit_length() - 1
    owned = CLUSTERS // peers
    slots = peers * cap
    ends = offsets(table_ref[...], peers) + table_ref[:peers]
    most_ref[...] = jnp.broadcast_to(jnp.max(ends, axis=(0, 1), keepdims=True), most_ref.shape)
    chosen = iota((LANES, CLUSTERS), 1) == (iota((LANES, CLUSTERS), 0) << bits) + me
    chosen = jnp.where(chosen, jnp.float32(1), jnp.float32(0))
    own = lax.dot_general(chosen, ends, NT, precision=EXACT, preferred_element_type=F32)
    own = jnp.where(iota(own.shape, 0) < owned, own, jnp.float32(1 << 20))

    index = iota((1, slots), 1)
    block = quotient(index, cap, slots)
    spot = (index - block * cap).astype(F32)
    from_peer = sender_of(me, block, peers) == iota((peers, slots), 0)
    from_peer = jnp.where(from_peer, jnp.float32(1), jnp.float32(0))
    ends = jnp.dot(own, from_peer, precision=EXACT, preferred_element_type=F32)
    row = jnp.sum(jnp.where(ends <= spot, 1.0, 0.0), axis=0, keepdims=True)
    row_ref[...] = row
    col_ref[...] = jnp.transpose(jnp.broadcast_to(row, (LANES, slots)))


def keys(me, table, cap):
    peers = table.shape[0] - 8
    slots = peers * cap
    return pl.pallas_call(
        functools.partial(key_kernel, cap),
        out_shape=(
            jax.ShapeDtypeStruct((1, slots), F32),
            jax.ShapeDtypeStruct((slots, LANES), F32),
            jax.ShapeDtypeStruct((8, LANES), F32),
        ),
        in_specs=[pl.BlockSpec(memory_space=pltpu.SMEM)] + whole(1),
        out_specs=tuple(whole(3)),
        cost_estimate=pl.CostEstimate(flops=1 << 36, bytes_accessed=1 << 22, transcendentals=0),
        compiler_params=pltpu.CompilerParams(vmem_limit_bytes=SMALL_VMEM),
        name="keys",
    )(me, table)


def rows_of(refs, cap, start, count):
    found, at = [], 0
    for ref in refs:
        blocks = ref.shape[0] // cap
        low, high = max(start, at), min(start + count, at + blocks)
        if low < high:
            found.append(ref[(low - at) * cap : (high - at) * cap, :])
        at += blocks
    return found[0] if len(found) == 1 else jnp.concatenate(found, axis=0)


def masked_parts(rows, columns, key_col, key_row, itself):
    gram = lax.dot_general(rows, columns, NT, preferred_element_type=F32)
    height, width = gram.shape
    parts = []
    for lane in range(0, width, LANES):
        wide = min(LANES, width - lane)
        part = gram[:, lane : lane + wide]
        keep = key_col[:, :wide] == key_row[:, lane : lane + wide]
        if -width < itself < height:
            keep = keep & (iota(part.shape, 0) - iota(part.shape, 1) != itself + lane)
        parts.append(jnp.where(keep, part, -1.0))
    return parts


def largest(parts):
    return jnp.concatenate([jnp.max(part, axis=0, keepdims=True) for part in parts], axis=1)


def first_kernel(cap, known, row_ref, col_ref, *refs):
    *block_refs, best_ref = refs
    tall, broad = max(1, 576 // cap), max(1, 432 // cap)
    for left in range(0, known, broad):
        count = min(broad, known - left)
        columns = rows_of(block_refs, cap, left, count)
        key_row = row_ref[:, left * cap : (left + count) * cap]
        best = jnp.full((1, count * cap), -1.0, F32)
        for upper in range(0, known, tall):
            rows = rows_of(block_refs, cap, upper, min(tall, known - upper))
            key_col = col_ref[upper * cap : upper * cap + rows.shape[0], :]
            best = jnp.maximum(best, largest(masked_parts(rows, columns, key_col, key_row, (left - upper) * cap)))
        for i in range(count):
            best_ref[left + i] = best[:, i * cap : (i + 1) * cap]


def next_kernel(cap, known, here, me_ref, row_ref, col_ref, before_ref, *refs):
    *block_refs, best_ref = refs
    me = me_ref[0]
    peers = row_ref.shape[1] // cap

    def place(block):
        return sender_of(me, block, peers) if here == peers else block

    tall = max(1, 576 // cap)
    columns = rows_of(block_refs, cap, known, here - known)
    key_row = row_ref[:, known * cap : here * cap]
    best = jnp.full((1, (here - known) * cap), -1.0, F32)
    for upper in range(0, here, tall):
        count = min(tall, here - upper)
        rows = rows_of(block_refs, cap, upper, count)
        key_col = col_ref[upper * cap : (upper + count) * cap, :]
        parts = masked_parts(rows, columns, key_col, key_row, (known - upper) * cap)
        best = jnp.maximum(best, largest(parts))
        if upper < known:
            tail = parts[-1]
            if tail.shape[1] < LANES:
                tail = jnp.concatenate([tail, jnp.full((count * cap, LANES - tail.shape[1]), -1.0, F32)], axis=1)
            side = functools.reduce(jnp.maximum, parts[:-1] + [tail])
            across = jnp.max(jnp.transpose(side), axis=0, keepdims=True)
            for i in range(min(count, known - upper)):
                found = jnp.maximum(before_ref[upper + i], across[:, i * cap : (i + 1) * cap])
                best_ref[place(upper + i)] = found
    for i in range(here - known):
        best_ref[place(known + i)] = best[:, i * cap : (i + 1) * cap]


def call_bests(kernel, scalars, arrays, blocks, out_blocks, fresh, cap):
    rows = sum(block.shape[0] for block in blocks)
    return pl.pallas_call(
        kernel,
        out_shape=jax.ShapeDtypeStruct((out_blocks, 1, cap), F32),
        in_specs=[pl.BlockSpec(memory_space=pltpu.SMEM)] * len(scalars) + whole(len(arrays) + len(blocks)),
        out_specs=whole(1)[0],
        cost_estimate=pl.CostEstimate(
            flops=2 * fresh * cap * rows * blocks[0].shape[1], bytes_accessed=1 << 23, transcendentals=0
        ),
        compiler_params=pltpu.CompilerParams(vmem_limit_bytes=VMEM_LIMIT),
        name="similar",
    )(*scalars, *arrays, *blocks)


def three_parts(values):
    high = values.astype(BF16)
    rest = values - high.astype(F32)
    middle = rest.astype(BF16)
    return high, middle, (rest - middle.astype(F32)).astype(BF16)


def result_kernel(dest_ref, back_ref, out_ref):
    peers, _, cap = back_ref.shape
    pieces = three_parts(back_ref[:, 0, :])
    step = 512
    for at in range(0, dest_ref.shape[1], step):
        dest = dest_ref[:, at : at + step]
        owner = dest // cap
        hot = one_hot(dest - owner * cap == iota((cap, step), 0))
        parts = [jnp.dot(part, hot, preferred_element_type=F32) for part in pieces]
        found = parts[0] + (parts[1] + parts[2])
        out_ref[:, at : at + step] = jnp.sum(jnp.where(owner == iota((peers, step), 0), found, 0.0), axis=0, keepdims=True)


def results(dest, back):
    return pl.pallas_call(
        result_kernel,
        out_shape=jax.ShapeDtypeStruct(dest.shape, F32),
        in_specs=whole(2),
        out_specs=whole(1)[0],
        compiler_params=pltpu.CompilerParams(vmem_limit_bytes=SMALL_VMEM),
        name="results",
    )(dest, back)


def cluster_best(pair):
    blocks, flags = pair
    peers, owned, most, width = blocks.shape
    slots = peers * most
    members = jnp.transpose(blocks, (1, 0, 2, 3)).reshape(owned, slots, width)
    valid = jnp.transpose(flags, (1, 0, 2)).reshape(owned, slots) > 0.5
    off_diagonal = jnp.logical_not(jnp.eye(slots, dtype=bool))

    def one_cluster(item):
        rows_of, valid_of = item
        gram = jnp.dot(rows_of, rows_of.T, preferred_element_type=jnp.float32)
        keep = valid_of[None, :] & off_diagonal
        return jnp.max(jnp.where(keep, gram, jnp.float32(-1.0)), axis=1)

    best = lax.map(one_cluster, (members, valid))
    return jnp.transpose(best.reshape(owned, peers, most), (1, 0, 2))


def roomy(labels, ranks, unit):
    count, width = unit.shape
    peers = lax.axis_size("rows")
    owned = CLUSTERS // peers
    cluster_hot = (labels[:, None] == jnp.arange(CLUSTERS, dtype=I32)[None, :]).astype(F32)
    rank_hot = (ranks[:, None] == jnp.arange(MOST, dtype=I32)[None, :]).astype(F32)
    numbered = rank_hot * jnp.arange(1, count + 1, dtype=F32)[:, None]
    filled = jnp.dot(cluster_hot.T, rank_hot, precision=EXACT)
    member_idx = jnp.dot(cluster_hot.T, numbered, precision=EXACT).astype(I32) - 1
    member_idx = jnp.where(member_idx < 0, count, member_idx).reshape(CLUSTERS * MOST)
    padded = jnp.concatenate([unit, jnp.zeros((1, width), BF16)], axis=0)
    outgoing = padded[member_idx].reshape(peers, owned, MOST, width)
    occupied = filled.astype(BF16).reshape(peers, owned, MOST)
    best = cluster_best((exchange(outgoing), exchange(occupied)))
    table = exchange(best).reshape(CLUSTERS, MOST)
    per_row = jnp.dot(cluster_hot, table, precision=EXACT)
    return jnp.sum(per_row * rank_hot, axis=1)


def exchange(blocks, groups=None):
    return lax.all_to_all(blocks, "rows", split_axis=0, concat_axis=0, tiled=True, axis_index_groups=groups)


def swap(block, number, peers):
    return lax.ppermute(block, "rows", [(i, i ^ number) for i in range(peers)])


def local(embeddings, cluster_id):
    count, width = embeddings.shape
    peers = lax.axis_size("rows")
    cap = -(-(count // peers + SLACK) // 16) * 16
    labels = cluster_id.reshape(1, count)
    counts = exchange(counted(labels, peers))
    ranks = ranked(labels)
    unit = unit_rows(embeddings)
    me = lax.axis_index("rows").reshape(1)

    half = peers // 2
    across = list(range(half, peers))
    dest, table, leaving = places_and_packed(me, counts, labels, ranks, unit, cap, across[:EARLY])
    later, _ = lax.optimization_barrier((dest, leaving[0]))
    leaving += list(packed(me, later, unit, cap, peers, across[EARLY:]))
    (inside,) = packed(me, later, unit, cap, peers, list(range(half)), half)
    arrived = [swap(block, number, peers) for block, number in zip(leaving, across)]
    inside, _, *arrived[:EARLY] = lax.optimization_barrier((inside, leaving[EARLY], *arrived[:EARLY]))
    inside = exchange(inside.reshape(half, cap, width), [list(range(half)), list(range(half, peers))])
    key_row, key_col, most = keys(me, table, cap)
    early = half - LATE
    blocks = arrived[:early] + [inside.reshape(half * cap, width)] + arrived[early:]
    first = functools.partial(first_kernel, cap, early)
    best = call_bests(first, [], [key_row, key_col], blocks[:early], early, early, cap)
    middle = functools.partial(next_kernel, cap, early, early + half)
    best = call_bests(middle, [me], [key_row, key_col, best], blocks[: early + 1], early + half, half, cap)
    last = functools.partial(next_kernel, cap, early + half, peers)
    best = call_bests(last, [me], [key_row, key_col, best], blocks, peers, LATE, cap)
    back = exchange(best)
    nearest = results(dest, back).reshape(count)
    return lax.cond(
        most[0, 0] > cap,
        lambda labels, ranks, unit, nearest: roomy(labels.reshape(count), ranks.reshape(count), unit),
        lambda labels, ranks, unit, nearest: nearest,
        labels, ranks, unit, nearest,
    )


def solution(mesh):
    return jax.shard_map(
        local,
        mesh=mesh,
        in_specs=(P(("groups", "rows"), None), P(("groups", "rows"), None)),
        out_specs=P(("groups", "rows")),
        check_vma=False,
    )
```
